256 devices in a mesh: seq: 32 (over x, y, core), tp: 8 (over z).
Axes of the slice: x: 4, y: 4, z: 8, core: 2. Of those that a mesh axis runs over, the one named last changes fastest.
Arguments:
- queries: bfloat16 [16384, 16, 128], P('seq', 'tp'), may hold values from -60 to 60
- keys: bfloat16 [16384, 8, 128], P('seq', 'tp'), may hold values from -60 to 60
- values: bfloat16 [16384, 8, 128], P('seq', 'tp'), may hold values from -5 to 5
- out_weight: bfloat16 [2048, 4608], P('tp'), may hold values from -0.125 to 0.125
- cotangent: bfloat16 [16384, 4608], P(('seq', 'tp')), may hold values from -5 to 5
- advantages: float32 [8], replicated, may hold values from -3 to 3
- lengths: int32 [8], replicated, may hold values from 1 to 6144, 16384 in all
Outputs:
- attention: bfloat16 [16384, 16, 128], P('seq', 'tp')
- d_queries: bfloat16 [16384, 16, 128], P('seq', 'tp')
- d_keys: bfloat16 [16384, 8, 128], P('seq', 'tp')
- d_values: bfloat16 [16384, 8, 128], P('seq', 'tp')
- d_wo_t: float32 [4608, 2048], P('seq', 'tp')
The draws below stay inside these ranges and needn't reach their ends.
Inputs may be any that keep to these rules, and one draw needn't show every extreme that they name: `lengths`: the rollouts lie one after another along the tokens and together fill all 16384.
All inputs are finite; a program needn't handle non-finite values.
Results may differ from the reference program's by a relative error of at most 0.028.
Values may be sent and summed in bfloat16 or wider, within the bound.
A program may use at most 128 MiB of HBM per device.

```python
import math
import jax
import jax.numpy as jnp
import numpy as np
from jax import lax

D = 4608
HEADS = 16
KV_HEADS = 8
HD = 128
WINDOW = 4096
TOK_DEV = 512
TOKENS = 16384
ROLLOUTS = 8
MOST = 6144


def draw_queries(key, part):
    shape = (TOKENS, HEADS, HD)
    result = jnp.clip(jax.random.normal(jax.random.fold_in(key, 21), shape, jnp.float32), -5.0, 5.0)
    return result.astype(jnp.bfloat16)


def draw_keys(key, part):
    shape = (TOKENS, KV_HEADS, HD)
    result = jnp.clip(jax.random.normal(jax.random.fold_in(key, 33), shape, jnp.float32), -5.0, 5.0)
    return result.astype(jnp.bfloat16)


def steps_of(rng, shape, pieces, least, largest):
    gain = 1.0
    for dim, parts in pieces:
        steps = jax.random.uniform(jax.random.fold_in(jax.random.fold_in(rng, 6), dim), (parts,), jnp.float32, least / len(pieces), largest / len(pieces))
        gain = gain * jnp.repeat(jnp.exp(steps), shape[dim] // parts).reshape((-1,) + (1,) * (len(shape) - 1 - dim))
    return gain


def profile(count, total, reach, lean):
    loads = [(1 << 20) // math.isqrt(rank ** lean) + 1 for rank in range(2, count + 1)]
    spare, holding = total - reach - (count - 1), [1] * (count - 1)
    while spare > 0:
        free = [i for i in range(count - 1) if holding[i] < reach]
        mass, budget = sum([loads[i] for i in free]), spare
        for i in free:
            extra = min(reach - holding[i], max(1, budget * loads[i] // mass), spare)
            holding[i] = holding[i] + extra
            spare = spare - extra
    return np.array([reach] + holding)


def ragged_sizes(own_key, amount, total, most, slope):
    if amount == 2:
        one = jax.random.randint(own_key, (), max(1, total - most), min(most, total - 1) + 1)
        return jnp.stack([one, total - one])
    sizes = jnp.asarray(profile(amount, total, most, slope), jnp.int32)
    twos = (amount - 1) // 2
    source_of, taker = sizes[1:1 + 2 * twos:2], sizes[2:2 + 2 * twos:2]
    room = jnp.minimum(source_of - 1, most - taker)
    shifted = jax.random.randint(jax.random.fold_in(own_key, 1), (twos,), 0, 1 << 20) % (room + 1)
    sizes = sizes.at[1:1 + 2 * twos:2].set(source_of - shifted).at[2:2 + 2 * twos:2].set(taker + shifted)
    return sizes[jax.random.permutation(jax.random.fold_in(own_key, 2), amount)]


def normal_values(own_key, extent, deviation, bound, cuts=(), held_as=jnp.bfloat16):
    values = deviation * jax.random.normal(own_key, extent, jnp.float32)
    if cuts:
        values = values * steps_of(own_key, extent, cuts, -0.22, 0.18)
    return jnp.clip(values, -bound, bound).astype(held_as)


def setup_inputs(seed: int = 0) -> dict:
    streams_of = jax.random.split(jax.random.key(seed), 8)
    return {
        "queries": draw_queries(jax.random.fold_in(streams_of[7], 71), 0),
        "keys": draw_keys(jax.random.fold_in(streams_of[7], 71), 0),
        "values": normal_values(streams_of[2], (TOKENS, KV_HEADS, HD), 1.0, 5.0, ((0, 32), (1, 8))),
        "out_weight": normal_values(streams_of[3], (HEADS * HD, D), (HEADS * HD) ** -0.5, 0.125, ((0, 8),)),
        "cotangent": normal_values(streams_of[4], (TOKENS, D), 1.0, 5.0, ((0, 256),)),
        "advantages": normal_values(streams_of[5], (ROLLOUTS,), 1.0, 3.0, (), jnp.float32),
        "lengths": ragged_sizes(streams_of[6], ROLLOUTS, TOKENS, MOST, 2).astype(jnp.int32),
    }


SCORE_SCALE = 1.0 / 12.0
MASKED_SCORE = -1.0e30


def rollout_index(lengths, places):
    finish = jnp.cumsum(lengths).astype(jnp.int32)
    return jnp.sum((finish[None, :] <= places[:, None]).astype(jnp.int32), axis=1).astype(jnp.int32)


def reference(queries, keys, values, out_weight, cotangent, advantages, lengths):
    total_rows = queries.shape[0]
    group_size = HEADS // KV_HEADS
    places = jnp.arange(total_rows, dtype=jnp.int32)
    rollout_ids = rollout_index(lengths, places)
    factors = advantages[rollout_ids]
    scaled = (factors[:, None] * cotangent.astype(jnp.float32)).astype(jnp.bfloat16)
    d_attn = jnp.dot(scaled, out_weight.T, preferred_element_type=jnp.float32).astype(jnp.bfloat16)
    d_attn = d_attn.reshape(total_rows, KV_HEADS, group_size, HD)
    grouped_q = queries.reshape(total_rows, KV_HEADS, group_size, HD)
    front_rows = jnp.zeros((WINDOW, KV_HEADS, HD), keys.dtype)
    padded_keys = jnp.concatenate([front_rows, keys], axis=0)
    padded_values = jnp.concatenate([front_rows, values], axis=0)
    padded_ids = jnp.concatenate([jnp.full((WINDOW,), -1, jnp.int32), rollout_ids], axis=0)
    query_block = min(TOK_DEV, 512)
    span_rows = WINDOW + query_block
    block_total = total_rows // query_block

    def one_block(carry, block_number):
        start = (block_number * query_block).astype(jnp.int32)
        q_block = lax.dynamic_slice_in_dim(grouped_q, start, query_block, 0).astype(jnp.float32)
        k_block = lax.dynamic_slice_in_dim(padded_keys, start, span_rows, 0).astype(jnp.float32)
        v_block = lax.dynamic_slice_in_dim(padded_values, start, span_rows, 0).astype(jnp.float32)
        d_block = lax.dynamic_slice_in_dim(d_attn, start, query_block, 0).astype(jnp.float32)
        query_ids = lax.dynamic_slice_in_dim(rollout_ids, start, query_block, 0)
        key_ids = lax.dynamic_slice_in_dim(padded_ids, start, span_rows, 0)
        query_places = start + jnp.arange(query_block, dtype=jnp.int32)
        key_places = start - WINDOW + jnp.arange(span_rows, dtype=jnp.int32)
        distance = query_places[:, None] - key_places[None, :]
        visible = (query_ids[:, None] == key_ids[None, :]) & (distance >= 0) & (distance < WINDOW)
        scores = jnp.einsum("tkgd,skd->kgts", q_block, k_block) * SCORE_SCALE
        masked = jnp.where(visible, scores, MASKED_SCORE)
        top = jnp.max(masked, axis=-1)
        weights = jnp.where(visible, jnp.exp(masked - top[..., None]), 0.0)
        log_total = top + jnp.log(jnp.sum(weights, axis=-1))
        probs = jnp.where(visible, jnp.exp(masked - log_total[..., None]), 0.0)
        probs_b = probs.astype(jnp.bfloat16)
        attn_block = jnp.einsum("kgts,skd->tkgd", probs_b.astype(jnp.float32), v_block).astype(jnp.bfloat16)
        delta = jnp.sum(d_block * attn_block.astype(jnp.float32), axis=-1)
        d_probs = jnp.einsum("tkgd,skd->kgts", d_block, v_block)
        d_scores = (probs * (d_probs - jnp.transpose(delta, (1, 2, 0))[..., None])).astype(jnp.bfloat16)
        d_scores_f = d_scores.astype(jnp.float32)
        dq_block = (jnp.einsum("kgts,skd->tkgd", d_scores_f, k_block) * SCORE_SCALE).astype(jnp.bfloat16)
        dk_part = jnp.einsum("kgts,tkgd->skd", d_scores_f, q_block) * SCORE_SCALE
        dv_part = jnp.einsum("kgts,tkgd->skd", probs_b.astype(jnp.float32), d_block)
        region = lax.dynamic_slice_in_dim(carry, start, span_rows, 0)
        carry = lax.dynamic_update_slice_in_dim(carry, region + jnp.concatenate([dk_part, dv_part], axis=-1), start, 0)
        return carry, (attn_block, dq_block)

    initial = jnp.zeros((WINDOW + total_rows, KV_HEADS, 2 * HD), jnp.float32)
    grads, outputs = lax.scan(one_block, initial, jnp.arange(block_total, dtype=jnp.int32))
    attention = outputs[0].reshape(total_rows, HEADS, HD)
    d_queries = outputs[1].reshape(total_rows, HEADS, HD)
    d_keys = grads[WINDOW:, :, :HD].astype(jnp.bfloat16)
    d_values = grads[WINDOW:, :, HD:].astype(jnp.bfloat16)
    d_wo_t = jnp.dot(scaled.T, attention.reshape(total_rows, HEADS * HD), preferred_element_type=jnp.float32)
    return (attention, d_queries, d_keys, d_values, d_wo_t)
```

```python
import functools
import math

import jax
import jax.numpy as jnp
from jax import lax
from jax.experimental import pallas as pl
from jax.experimental.pallas import tpu as pltpu
from jax.sharding import PartitionSpec as P

WINDOW = 4096
SIDE = 4
RING = 8
BACK = 8
SCALE = 1.0 / 12.0
EXP2_SCALE = SCALE * math.log2(math.e)
MASKED = -1e30
BF = jnp.bfloat16
F32 = jnp.float32
MESH = pl.DeviceIdType.MESH
NN = (((1,), (0,)), ((), ()))
NT = (((1,), (1,)), ((), ()))
TN = (((0,), (0,)), ((), ()))


def dot(a, b, dims):
    return lax.dot_general(a, b, dims, preferred_element_type=F32)


def kernel(
    lens, adv, q_ref, k_ref, v_ref, w_hbm, cot_ref,
    att_o, dq_o, dk_o, dv_o, dwo_o,
    sc, w, kv, q2, qT, lo, S, Pb, mx, rl, O2, att2,
    dA, dAs, dAsT, delta, dq, dS,
    dwf, psend, precv, ysend, yrecv, xsend, xrecv, xown,
    ssend, srecv, rsend, rrecv, lsend, lrecv,
    gs_sem, gr_sem, w_sem, hx_sem, hy_sem, hs_sem,
    pp_sem, yy_sem, xs_sem, xr_sem, ss_sem, rr_sem, ll_sem,
):
    s = lax.axis_index("seq")
    z = lax.axis_index("tp")
    core = lax.rem(s, 2)
    chip = s // 2
    y = lax.rem(chip, SIDE)
    x = chip // SIDE
    rows, fs = sc.shape[1], sc.shape[2]
    ebuf = S.at[:, : 2 * k_ref.shape[1], :]
    slices = sc.shape[0]
    part = rows // RING
    hd = k_ref.shape[1]
    own_rows = dwo_o.shape[0]

    def row_dev(i):
        return {"seq": x * (2 * SIDE) + lax.rem(y + i + SIDE, SIDE) * 2 + core}

    def col_dev(i):
        return {"seq": lax.rem(x + i + SIDE, SIDE) * (2 * SIDE) + y * 2 + core}

    def ring_dev(i):
        return {"tp": lax.rem(z + i + RING, RING)}

    sib_dev = {"seq": s + 1 - 2 * core}

    def remote(src, dst, send, recv, dev):
        return pltpu.make_async_remote_copy(
            src_ref=src, dst_ref=dst, send_sem=send, recv_sem=recv, device_id=dev, device_id_type=MESH
        )

    barrier = pltpu.get_barrier_semaphore()
    for dev in [sib_dev, ring_dev(1), ring_dev(-1)] + [f(i) for f in (row_dev, col_dev) for i in (1, 2, 3)]:
        pl.semaphore_signal(barrier, inc=1, device_id=dev, device_id_type=MESH)
    w_copy = pltpu.make_async_copy(w_hbm, w, w_sem)
    w_copy.start()

    place = s * rows + z * part + lax.broadcasted_iota(jnp.int32, (part, hd), 0)
    factor = jnp.full((part, hd), adv[0], F32)
    cum = jnp.int32(0)
    for r in range(lens.shape[0] - 1):
        cum = cum + lens[r]
        factor = jnp.where(place >= cum, adv[r + 1], factor)
    wide = jnp.concatenate([factor] * (fs // hd), axis=1)
    my_rows = pl.ds(pl.multiple_of(z * part, part), part)
    for f in range(slices):
        piece = cot_ref[:, f * fs : (f + 1) * fs].astype(F32)
        sc[f, my_rows, :] = (wide * piece).astype(BF)
    kv[0, :, :hd] = k_ref[...]
    kv[0, :, hd:] = v_ref[...]

    pl.semaphore_wait(barrier, 9)

    def chunk_rows(sign, away, kind):
        chunk = lax.rem(z - sign * away + RING, RING)
        half = part // 2
        if kind < 3:
            return pl.ds(pl.multiple_of(chunk * part, part), part)
        return pl.ds(pl.multiple_of(chunk * part + (0 if sign > 0 else half), half), half)

    def ring_copy(way, kind, f, away):
        sign = 1 - 2 * way
        ref = sc.at[f, chunk_rows(sign, away, kind)]
        return remote(ref, ref, gs_sem.at[way, kind, f], gr_sem.at[way, kind, f], ring_dev(sign))

    def arrived(kind, f):
        for way in (0, 1):
            ring_copy(way, kind, f, kind + 1).wait_recv()

    def event(kind, f):
        if kind:
            arrived(kind - 1, f)
        for way in (0, 1):
            ring_copy(way, kind, f, kind).start()

    event(0, 0)
    event(0, 1)

    hx = remote(kv.at[0], kv.at[8], hx_sem.at[0], hx_sem.at[1], col_dev(1))
    hx.start()

    def hy(i, slot):
        return remote(kv.at[slot], kv.at[2 * i], hy_sem.at[0, i], hy_sem.at[1, i], row_dev(i))

    def hs(j):
        return remote(
            kv.at[2 * (j - 1 + core)], kv.at[2 * j - 1], hs_sem.at[0, j], hs_sem.at[1, j], sib_dev
        )

    for i in (1, 2, 3):
        @pl.when(y + i < SIDE)
        def _():
            hy(i, 0).start()

    @pl.when(core == 0)
    def _():
        hs(1).start()

    q2[:rows, :] = q_ref[:, 0, :]
    q2[rows:, :] = q_ref[:, 1, :]
    qT[...] = q2[...].astype(F32).T.astype(BF)
    place = s * rows + lax.broadcasted_iota(jnp.int32, (rows, hd), 0)
    first = jnp.zeros((rows, hd), jnp.int32)
    cum = jnp.int32(0)
    for r in range(lens.shape[0] - 1):
        cum = cum + lens[r]
        first = jnp.where(place >= cum, cum, first)
    lo[...] = jnp.maximum(first, place - (WINDOW - 1)) - s * rows

    tile = 256
    tiles = 2 * rows // tile
    per_head = rows // tile

    def tile_rows(r):
        return pl.ds(pl.multiple_of(r * tile, tile), tile)

    def scores(d):
        def step(r, carry):
            at = tile_rows(r)
            raw = dot(q2[at, :], kv[d, :, :hd], NT)
            t0 = lax.rem(r, per_head) * tile
            low = lo[pl.ds(pl.multiple_of(t0, tile), tile), :] + d * rows
            best = None
            for c in range(rows // hd):
                col = lax.broadcasted_iota(jnp.int32, (tile, hd), 1) + c * hd
                seen = col >= low
                if d == 0:
                    seen = seen & (col <= lax.broadcasted_iota(jnp.int32, (tile, hd), 0) + t0)
                val = jnp.where(seen, raw[:, c * hd : (c + 1) * hd], MASKED)
                S[d, at, c * hd : (c + 1) * hd] = val
                best = val if best is None else jnp.maximum(best, val)
            mx[at, :] = best if d == 0 else jnp.maximum(mx[at, :], best)
            return carry

        lax.fori_loop(0, tiles, step, 0)

    def weigh(r):
        at = pl.ds(r * tile, tile)
        top = jnp.broadcast_to(jnp.max(mx[at, :], axis=1, keepdims=True), (tile, hd))
        mx[at, :] = top
        rl[at, :] = jnp.zeros((tile, hd), F32)
        O2[at, :] = jnp.zeros((tile, hd), F32)

        def step(d, carry):
            top = mx[at, :]
            total = rl[at, :]
            for c in range(rows // hd):
                p = jnp.exp2((S[d, at, c * hd : (c + 1) * hd] - top) * EXP2_SCALE)
                total = total + p
                Pb[d, at, c * hd : (c + 1) * hd] = p.astype(BF)
            rl[at, :] = total
            O2[at, :] += dot(Pb[d, at, :], kv[d, :, hd:], NN)
            return carry

        lax.fori_loop(0, BACK + 1, step, 0)
        inv = 1.0 / jnp.broadcast_to(jnp.sum(rl[at, :], axis=1, keepdims=True), (tile, hd))
        rl[at, :] = inv
        out = (O2[at, :] * inv).astype(BF)
        att2[at, :] = out
        t0, h = (r % per_head) * tile, r // per_head
        att_o[t0 : t0 + tile, h * hd : (h + 1) * hd] = out

    def project(f):
        term = dot(sc[f], w[:, f * fs : (f + 1) * fs], NT)
        if f == 0:
            dA[...] = term
        else:
            dA[...] += term

    def pair_copy(f):
        return remote(psend.at[f], precv.at[f], pp_sem.at[0, f], pp_sem.at[1, f], sib_dev)

    def weight_grad(f):
        def step(i, carry):
            at = pl.ds(pl.multiple_of(i * hd, hd), hd)
            dwf[f, at, :] = dot(sc[f, :, at], att_o[...], TN)
            return carry

        for i in range(fs // hd):
            step(i, 0)
        for j in range(SIDE):
            theirs = pl.ds(pl.multiple_of((2 * j + 1 - core) * own_rows, own_rows), own_rows)
            psend[f, j] = dwf[f, theirs, :].astype(BF)
        pair_copy(f).start()

    def pair_sum(f, j):
        mine = pl.ds(pl.multiple_of((2 * j + core) * own_rows, own_rows), own_rows)
        return dwf[f, mine, :] + precv[f, j].astype(F32)

    def row_copy(f, i):
        return remote(ysend.at[f, i], yrecv.at[f, i], yy_sem.at[0, f, i], yy_sem.at[1, f, i], row_dev(i))

    def row_send(f):
        pair_copy(f).wait_recv()
        for i in (1, 2, 3):
            ysend[f, i] = pair_sum(f, lax.rem(y + i, SIDE)).astype(BF)
            row_copy(f, i).start()

    def col_copy(f):
        slot = lax.rem(x - f + SIDE, SIDE)
        return remote(
            xsend.at[f], xrecv.at[slot], xs_sem.at[f], xr_sem.at[slot],
            {"seq": f * (2 * SIDE) + y * 2 + core},
        )

    def col_send(f):
        total = pair_sum(f, y)
        for i in (1, 2, 3):
            row_copy(f, i).wait_recv()
            total = total + yrecv[f, i].astype(F32)

        @pl.when(x == f)
        def _():
            xown[...] = total

        @pl.when(x != f)
        def _():
            xsend[f] = total.astype(BF)
            col_copy(f).start()

    def backward(d, out):
        for r in range(tiles):
            at = pl.ds(r * tile, tile)
            raw = dot(dAs[at, :], kv[d, :, hd:], NT)
            low = delta[at, :]
            for c in range(rows // hd):
                cs = slice(c * hd, (c + 1) * hd)
                dS[at, cs] = (Pb[d, at, cs].astype(F32) * (raw[:, cs] - low)).astype(BF)
            term = dot(dS[at, :], kv[d, :, :hd], NN)
            if d == BACK - 1:
                dq[at, :] = term
            else:
                dq[at, :] += term
        out[:hd, :] = dot(qT[...], dS[...], NN).astype(out.dtype)
        out[hd:, :] = dot(dAsT[...], Pb[d], NN).astype(out.dtype)

    def sib_copy(i):
        return remote(ssend.at[i], srecv.at[i], ss_sem.at[0, i], ss_sem.at[1, i], sib_dev)

    def back_copy(i):
        return remote(rsend.at[i], rrecv.at[i], rr_sem.at[0, i], rr_sem.at[1, i], row_dev(-i))

    relay = remote(lsend, lrecv, ll_sem.at[0], ll_sem.at[1], col_dev(-1))

    def odd(i):
        backward(2 * i - 1, ssend.at[i])
        sib_copy(i).start()

    def send_back(i):
        rsend[i] = (ebuf[i] + srecv[i + 1 - core].astype(F32)).astype(BF)
        back_copy(i).start()

    scores(0)
    event(1, 0)
    event(0, 2)
    hx.wait_recv()
    for i in (1, 2, 3):
        @pl.when(y + i >= SIDE)
        def _():
            hy(i, 8).start()
    scores(8)
    w_copy.wait()
    event(2, 0)
    event(1, 1)
    for j in (1, 2, 3, 4):
        if j < 4:
            hy(j, 0).wait_recv()
        if j == 1:
            @pl.when(core == 1)
            def _():
                hs(1).start()
        else:
            hs(j).start()
        if j < 4:
            scores(2 * j)
        hs(j).wait_recv()
        scores(2 * j - 1)
        if j == 3:
            event(3, 0)
    weigh(0)
    event(2, 1)
    event(0, 3)
    weigh(1)
    weigh(2)
    event(1, 2)
    weigh(3)
    event(3, 1)
    arrived(3, 0)
    project(0)
    weight_grad(0)
    event(2, 2)
    event(1, 3)
    arrived(3, 1)
    project(1)
    weight_grad(1)
    row_send(0)
    event(3, 2)
    event(2, 3)
    col_send(0)
    row_send(1)
    arrived(3, 2)
    project(2)
    weight_grad(2)
    event(3, 3)
    col_send(1)
    row_send(2)
    arrived(3, 3)
    project(3)

    for h in range(2):
        hr = slice(h * rows, (h + 1) * rows)
        rounded = dA[:, h * hd : (h + 1) * hd].astype(BF).astype(F32)
        scaled = (rounded * rl[hr, :]).astype(BF)
        dAs[hr, :] = scaled
        wide = scaled.astype(F32)
        dAsT[:, hr] = wide.T.astype(BF)
        d = jnp.sum(wide * att2[hr, :].astype(F32), axis=1, keepdims=True)
        delta[hr, :] = jnp.broadcast_to(d, (rows, hd))

    odd(4)
    weight_grad(3)
    odd(3)
    backward(6, ebuf.at[3])
    col_send(2)
    sib_copy(4).wait_recv()
    sib_copy(3).wait_recv()
    send_back(3)
    odd(2)
    row_send(3)
    backward(4, ebuf.at[2])
    sib_copy(2).wait_recv()
    send_back(2)
    odd(1)
    backward(2, ebuf.at[1])
    sib_copy(1).wait_recv()
    send_back(1)
    col_send(3)
    backward(8, ebuf.at[4])
    total = ebuf[4] + jnp.where(core == 1, srecv[4].astype(F32), 0.0)
    for i in (3, 2, 1):
        back_copy(i).wait_recv()
        total = total + jnp.where(y + i >= SIDE, rrecv[i].astype(F32), 0.0)
    lsend[...] = total.astype(BF)
    relay.start()
    backward(0, ebuf.at[0])
    for h in range(2):
        hr = slice(h * rows, (h + 1) * rows)
        dq_o[:, h * hd : (h + 1) * hd] = (dq[hr, :] * SCALE).astype(BF)
    own = xown[...]
    for i in (1, 2, 3):
        remote(xsend.at[i], xrecv.at[i], xs_sem.at[i], xr_sem.at[i], col_dev(i)).wait_recv()
        own = own + xrecv[i].astype(F32)
    dwo_o[...] = own
    total = ebuf[0] + jnp.where(core == 0, srecv[1].astype(F32), 0.0)
    for i in (1, 2, 3):
        total = total + jnp.where(y + i < SIDE, rrecv[i].astype(F32), 0.0)
    relay.wait_recv()
    total = total + lrecv[...].astype(F32)
    dk_o[...] = (total[:hd, :].T * SCALE).astype(BF)
    dv_o[...] = total[hd:, :].T.astype(BF)

    for f in range(slices):
        for way in (0, 1):
            for kind in range(4):
                ring_copy(way, kind, f, kind).wait_send()
        pair_copy(f).wait_send()
        for i in (1, 2, 3):
            row_copy(f, i).wait_send()

        @pl.when(x != f)
        def _():
            col_copy(f).wait_send()
    hx.wait_send()
    for i in (1, 2, 3):
        hy(i, 0).wait_send()
        back_copy(i).wait_send()
    for i in (1, 2, 3, 4):
        hs(i).wait_send()
        sib_copy(i).wait_send()
    relay.wait_send()


def per_device(queries, keys, values, out_weight, cotangent, advantages, lengths):
    rows, heads, hd = queries.shape
    width = heads * hd
    depth = cotangent.shape[1]
    slices = SIDE
    fs = depth // slices
    own = depth // lax.axis_size("seq")
    q_rows = heads * rows
    vmem = pl.BlockSpec(memory_space=pltpu.VMEM)
    smem = pl.BlockSpec(memory_space=pltpu.SMEM)
    dma = pltpu.SemaphoreType.DMA
    V = pltpu.VMEM
    out = pl.pallas_call(
        kernel,
        out_shape=[
            jax.ShapeDtypeStruct((rows, width), BF),
            jax.ShapeDtypeStruct((rows, width), BF),
            jax.ShapeDtypeStruct((rows, hd), BF),
            jax.ShapeDtypeStruct((rows, hd), BF),
            jax.ShapeDtypeStruct((own, width), F32),
        ],
        in_specs=[smem, smem, vmem, vmem, vmem, pl.BlockSpec(memory_space=pl.ANY), vmem],
        out_specs=[vmem] * 5,
        scratch_shapes=[
            V((slices, rows, fs), BF),
            V((width, depth), BF),
            V((BACK + 1, rows, 2 * hd), BF),
            V((q_rows, hd), BF),
            V((hd, q_rows), BF),
            V((rows, hd), jnp.int32),
            V((BACK + 1, q_rows, rows), F32),
            V((BACK + 1, q_rows, rows), BF),
            V((q_rows, hd), F32),
            V((q_rows, hd), F32),
            V((q_rows, hd), F32),
            V((q_rows, hd), BF),
            V((rows, width), F32),
            V((q_rows, hd), BF),
            V((hd, q_rows), BF),
            V((q_rows, hd), F32),
            V((q_rows, hd), F32),
            V((q_rows, rows), BF),
            V((slices, fs, width), F32),
            V((slices, SIDE, own, width), BF),
            V((slices, SIDE, own, width), BF),
            V((slices, SIDE, own, width), BF),
            V((slices, SIDE, own, width), BF),
            V((slices, own, width), BF),
            V((SIDE, own, width), BF),
            V((own, width), F32),
            V((5, 2 * hd, rows), BF),
            V((5, 2 * hd, rows), BF),
            V((4, 2 * hd, rows), BF),
            V((4, 2 * hd, rows), BF),
            V((2 * hd, rows), BF),
            V((2 * hd, rows), BF),
            dma((2, 4, slices)),
            dma((2, 4, slices)),
            dma,
            dma((2,)),
            dma((2, 4)),
            dma((2, 5)),
            dma((2, slices)),
            dma((2, slices, 4)),
            dma((slices,)),
            dma((4,)),
            dma((2, 5)),
            dma((2, 4)),
            dma((2,)),
        ],
        compiler_params=pltpu.CompilerParams(
            collective_id=0, has_side_effects=True, vmem_limit_bytes=60 * 1024 * 1024
        ),
        cost_estimate=pl.CostEstimate(flops=9 * 10**9, bytes_accessed=5 * 10**6, transcendentals=5 * 10**6),
        name="rollout_attention",
    )(lengths, advantages, queries, keys.reshape(rows, hd), values.reshape(rows, hd), out_weight, cotangent)
    attention, d_queries, d_keys, d_values, d_weight = out
    return (
        attention.reshape(rows, heads, hd),
        d_queries.reshape(rows, heads, hd),
        d_keys.reshape(rows, 1, hd),
        d_values.reshape(rows, 1, hd),
        d_weight,
    )


def solution(mesh):
    tokens = P("seq", "tp", None)
    return jax.shard_map(
        per_device,
        mesh=mesh,
        in_specs=(tokens, tokens, tokens, P("tp", None), P(("seq", "tp"), None), P(), P()),
        out_specs=(tokens, tokens, tokens, tokens, P("seq", "tp")),
        check_vma=False,
    )
```

```python
import functools
import math

import jax
import jax.numpy as jnp
from jax import lax
from jax.experimental import pallas as pl
from jax.experimental.pallas import tpu as pltpu
from jax.sharding import PartitionSpec as P

WINDOW = 4096
SIDE = 4
RING = 8
BACK = 8
SCALE = 1.0 / 12.0
EXP2_SCALE = SCALE * math.log2(math.e)
MASKED = -1e30
BF = jnp.bfloat16
F32 = jnp.float32
MESH = pl.DeviceIdType.MESH
NN = (((1,), (0,)), ((), ()))
NT = (((1,), (1,)), ((), ()))
TN = (((0,), (0,)), ((), ()))


def dot(a, b, dims):
    return lax.dot_general(a, b, dims, preferred_element_type=F32)


def kernel(
    lens, adv, q_ref, k_ref, v_ref, w_hbm, cot_ref,
    att_o, dq_o, dk_o, dv_o, dwo_o,
    sc, w, kv, q2, qT, lo, S, Pb, mx, rl, O2, att2,
    dA, dAs, dAsT, delta, dq, dS,
    psend, precv, ysend, yrecv, yown, xsend, xrecv, xown,
    ssend, srecv, rsend, rrecv, lsend, lrecv,
    gs_sem, gr_sem, w_sem, hx_sem, hy_sem, hs_sem,
    pp_sem, yy_sem, xs_sem, xr_sem, ss_sem, rr_sem, ll_sem,
):
    s = lax.axis_index("seq")
    z = lax.axis_index("tp")
    core = lax.rem(s, 2)
    chip = s // 2
    y = lax.rem(chip, SIDE)
    x = chip // SIDE
    rows, fs = sc.shape[1], sc.shape[2]
    ebuf = S.at[:, : 2 * k_ref.shape[1], :]
    slices = sc.shape[0]
    part = rows // RING
    hd = k_ref.shape[1]
    own_rows = dwo_o.shape[0]

    def row_dev(i):
        return {"seq": x * (2 * SIDE) + lax.rem(y + i + SIDE, SIDE) * 2 + core}

    def col_dev(i):
        return {"seq": lax.rem(x + i + SIDE, SIDE) * (2 * SIDE) + y * 2 + core}

    def ring_dev(i):
        return {"tp": lax.rem(z + i + RING, RING)}

    sib_dev = {"seq": s + 1 - 2 * core}

    def remote(src, dst, send, recv, dev):
        return pltpu.make_async_remote_copy(
            src_ref=src, dst_ref=dst, send_sem=send, recv_sem=recv, device_id=dev, device_id_type=MESH
        )

    barrier = pltpu.get_barrier_semaphore()
    next_dev = {"seq": lax.rem(s + 2, 2 * SIDE * SIDE)}
    last_dev = {"seq": lax.rem(s - 2 + 2 * SIDE * SIDE, 2 * SIDE * SIDE)}
    around = [f(i) for f in (row_dev, col_dev) for i in (1, 2, 3)]
    for dev in [sib_dev, ring_dev(1), ring_dev(-1), next_dev] + around:
        pl.semaphore_signal(barrier, inc=1, device_id=dev, device_id_type=MESH)
    w_copy = pltpu.make_async_copy(w_hbm, w, w_sem)
    w_copy.start()

    place = s * rows + z * part + lax.broadcasted_iota(jnp.int32, (part, hd), 0)
    factor = jnp.full((part, hd), adv[0], F32)
    cum = jnp.int32(0)
    for r in range(lens.shape[0] - 1):
        cum = cum + lens[r]
        factor = jnp.where(place >= cum, adv[r + 1], factor)
    wide = jnp.concatenate([factor] * (fs // hd), axis=1)
    my_rows = pl.ds(pl.multiple_of(z * part, part), part)
    for f in range(slices):
        piece = cot_ref[:, f * fs : (f + 1) * fs].astype(F32)
        sc[f, my_rows, :] = (wide * piece).astype(BF)
    kv[0, :, :hd] = k_ref[...]
    kv[0, :, hd:] = v_ref[...]

    pl.semaphore_wait(barrier, 10)

    def chunk_rows(sign, away, kind):
        chunk = lax.rem(z - sign * away + RING, RING)
        half = part // 2
        if kind < 3:
            return pl.ds(pl.multiple_of(chunk * part, part), part)
        return pl.ds(pl.multiple_of(chunk * part + (0 if sign > 0 else half), half), half)

    def ring_copy(way, kind, f, away):
        sign = 1 - 2 * way
        ref = sc.at[f, chunk_rows(sign, away, kind)]
        return remote(ref, ref, gs_sem.at[way, kind, f], gr_sem.at[way, kind, f], ring_dev(sign))

    def arrived(kind, f):
        for way in (0, 1):
            ring_copy(way, kind, f, kind + 1).wait_recv()

    def event(kind, f):
        if kind:
            arrived(kind - 1, f)
        for way in (0, 1):
            ring_copy(way, kind, f, kind).start()

    event(0, 0)
    event(0, 1)

    def hx():
        return remote(kv.at[0], kv.at[8], hx_sem.at[0], hx_sem.at[1], col_dev(1))

    hx().start()

    def hy(i, slot):
        return remote(kv.at[slot], kv.at[2 * i], hy_sem.at[0, i], hy_sem.at[1, i], row_dev(i))

    def hs(i):
        j = i + 1 - core
        return remote(kv.at[2 * i], kv.at[2 * j - 1], hs_sem.at[0, j], hs_sem.at[1, j], sib_dev)

    def hs_from(j):
        return remote(kv.at[2 * j], kv.at[2 * j - 1], hs_sem.at[0, j], hs_sem.at[1, j], sib_dev)

    for i in (1, 2, 3):
        @pl.when(y + i < SIDE)
        def _():
            hy(i, 0).start()

    @pl.when(core == 0)
    def _():
        hs(0).start()

    q2[:rows, :] = q_ref[:, 0, :]
    q2[rows:, :] = q_ref[:, 1, :]
    qT[...] = q2[...].astype(F32).T.astype(BF)
    place = s * rows + lax.broadcasted_iota(jnp.int32, (rows, hd), 0)
    first = jnp.zeros((rows, hd), jnp.int32)
    cum = jnp.int32(0)
    for r in range(lens.shape[0] - 1):
        cum = cum + lens[r]
        first = jnp.where(place >= cum, cum, first)
    lo[...] = jnp.maximum(first, place - (WINDOW - 1)) - s * rows

    tile = 256
    tiles = 2 * rows // tile
    per_head = rows // tile

    def tile_rows(r):
        return pl.ds(pl.multiple_of(r * tile, tile), tile)

    def scores(d):
        def step(r, carry):
            at = tile_rows(r)
            raw = dot(q2[at, :], kv[d, :, :hd], NT)
            t0 = lax.rem(r, per_head) * tile
            low = lo[pl.ds(pl.multiple_of(t0, tile), tile), :] + d * rows
            best = None
            for c in range(rows // hd):
                col = lax.broadcasted_iota(jnp.int32, (tile, hd), 1) + c * hd
                seen = col >= low
                if d == 0:
                    seen = seen & (col <= lax.broadcasted_iota(jnp.int32, (tile, hd), 0) + t0)
                val = jnp.where(seen, raw[:, c * hd : (c + 1) * hd], MASKED)
                S[d, at, c * hd : (c + 1) * hd] = val
                best = val if best is None else jnp.maximum(best, val)
            mx[at, :] = best if d == 0 else jnp.maximum(mx[at, :], best)
            return carry

        lax.fori_loop(0, tiles, step, 0)

    def weigh(r, last):
        at = pl.ds(r * tile, tile)
        if not last:
            mx[at, :] = jnp.broadcast_to(jnp.max(mx[at, :], axis=1, keepdims=True), (tile, hd))
            rl[at, :] = jnp.zeros((tile, hd), F32)
            O2[at, :] = jnp.zeros((tile, hd), F32)

        def step(d, carry):
            top = mx[at, :]
            total = rl[at, :]
            for c in range(rows // hd):
                p = jnp.exp2((S[d, at, c * hd : (c + 1) * hd] - top) * EXP2_SCALE)
                total = total + p
                Pb[d, at, c * hd : (c + 1) * hd] = p.astype(BF)
            rl[at, :] = total
            O2[at, :] += dot(Pb[d, at, :], kv[d, :, hd:], NN)
            return carry

        middle = BACK // 2
        if not last:
            lax.fori_loop(0, middle, step, 0)
            return
        lax.fori_loop(middle, BACK + 1, step, 0)
        inv = 1.0 / jnp.broadcast_to(jnp.sum(rl[at, :], axis=1, keepdims=True), (tile, hd))
        rl[at, :] = inv
        out = (O2[at, :] * inv).astype(BF)
        att2[at, :] = out
        t0, h = (r % per_head) * tile, r // per_head
        att_o[t0 : t0 + tile, h * hd : (h + 1) * hd] = out

    def project(f):
        term = dot(sc[f], w[:, f * fs : (f + 1) * fs], NT)
        if f == 0:
            dA[...] = term
        else:
            dA[...] += term

    def pair_copy(f):
        return remote(psend.at[f], precv.at[f], pp_sem.at[0, f], pp_sem.at[1, f], sib_dev)

    def weight_rows(f, j, which):
        width = att_o.shape[1]
        at = pl.ds(pl.multiple_of((2 * (j % 2) + which) * own_rows, own_rows), own_rows)
        return S[BACK - f, at, (j // 2) * width : (j // 2 + 1) * width]

    def weight_grad(f):
        width = att_o.shape[1]
        cut = fs // 2
        for i in range(fs // hd):
            term = dot(sc[f, :, i * hd : (i + 1) * hd], att_o[...], TN)
            for side in (0, 1):
                first, last = max(i * hd, side * cut), min((i + 1) * hd, (side + 1) * cut)
                if first < last:
                    S[BACK - f, first - side * cut : last - side * cut, pl.ds(side * width, width)] = (
                        term[first - i * hd : last - i * hd]
                    )
        for j in range(SIDE):
            psend[f, j] = weight_rows(f, j, 1 - core).astype(BF)
        pair_copy(f).start()

    def row_copy(f, i):
        return remote(ysend.at[f, i], yrecv.at[f, i], yy_sem.at[0, f, i], yy_sem.at[1, f, i], row_dev(i))

    def row_send(f):
        pair_copy(f).wait_recv()
        for j in range(SIDE):
            both = weight_rows(f, j, core) + precv[f, j].astype(F32)
            ysend[f, lax.rem(j - y + SIDE, SIDE)] = both.astype(BF)

            @pl.when(y == j)
            def _():
                yown[f] = both

        for i in (1, 2, 3):
            row_copy(f, i).start()

    def col_copy(f):
        slot = lax.rem(x - f + SIDE, SIDE)
        return remote(
            xsend.at[f], xrecv.at[slot], xs_sem.at[f], xr_sem.at[slot],
            {"seq": f * (2 * SIDE) + y * 2 + core},
        )

    def col_from(i):
        return remote(xsend.at[i], xrecv.at[i], xs_sem.at[i], xr_sem.at[i], col_dev(i))

    def col_send(f):
        total = yown[f]
        for i in (1, 2, 3):
            row_copy(f, i).wait_recv()
            total = total + yrecv[f, i].astype(F32)

        @pl.when(x == f)
        def _():
            xown[...] = total

        @pl.when(x != f)
        def _():
            xsend[f] = total.astype(BF)
            col_copy(f).start()

    def backward(d, out, first=False):
        for r in range(tiles):
            at = pl.ds(r * tile, tile)
            raw = dot(dAs[at, :], kv[d, :, hd:], NT)
            low = delta[at, :]
            for c in range(rows // hd):
                cs = slice(c * hd, (c + 1) * hd)
                dS[at, cs] = (Pb[d, at, cs].astype(F32) * (raw[:, cs] - low)).astype(BF)
            term = dot(dS[at, :], kv[d, :, :hd], NN)
            if first:
                dq[at, :] = term
            else:
                dq[at, :] += term
        out[:hd, :] = dot(qT[...], dS[...], NN).astype(out.dtype)
        out[hd:, :] = dot(dAsT[...], Pb[d], NN).astype(out.dtype)

    def sib_copy(i):
        return remote(ssend.at[i], srecv.at[i], ss_sem.at[0, i], ss_sem.at[1, i], sib_dev)

    def half(ref, h):
        return ref.at[pl.ds(h * hd, hd)]

    def back_copy(i, h):
        dev = last_dev if i == 1 else row_dev(-i)
        return remote(half(rsend.at[i], h), half(rrecv.at[i], h), rr_sem.at[0, i, h], rr_sem.at[1, i, h], dev)

    def relay(h):
        return remote(half(lsend, h), half(lrecv, h), ll_sem.at[0, h], ll_sem.at[1, h], col_dev(-1))

    def odd(i, first=False):
        backward(2 * i - 1, ssend.at[i], first)
        sib_copy(i).start()

    def send_back(i):
        j = i + 1 - core
        sib_copy(j).wait_recv()
        for h in (0, 1):
            hs_ = pl.ds(h * hd, hd)
            rsend[i, hs_, :] = (ebuf[i, hs_, :] + srecv[j, hs_, :].astype(F32)).astype(BF)
            back_copy(i, h).start()

    def relay_in():
        hx().wait_recv()
        for i in (1, 2, 3):
            @pl.when(y + i >= SIDE)
            def _():
                hy(i, 8).start()

        @pl.when(core == 1)
        def _():
            hs(4).start()

    def even_in(i):
        hy(i, 0).wait_recv()
        hs(i).start()
        scores(2 * i)

    def odd_in(j):
        hs_from(j).wait_recv()
        scores(2 * j - 1)

    scores(0)
    event(1, 0)
    event(0, 2)
    relay_in()
    scores(8)
    event(1, 1)
    event(2, 0)
    even_in(1)
    event(2, 1)
    event(1, 2)
    odd_in(1)
    even_in(3)
    event(3, 0)
    event(0, 3)
    even_in(2)
    odd_in(2)
    odd_in(3)
    event(3, 1)
    odd_in(4)
    weigh(0, False)
    weigh(0, True)
    event(2, 2)
    weigh(1, False)
    weigh(1, True)
    w_copy.wait()
    arrived(3, 0)
    project(0)
    weigh(2, False)
    weigh(2, True)
    event(1, 3)
    weigh(3, False)
    arrived(3, 1)
    project(1)
    weigh(3, True)
    weight_grad(0)
    event(3, 2)

    weight_grad(1)
    row_send(0)
    event(2, 3)
    row_send(1)
    arrived(3, 2)
    project(2)
    weight_grad(2)
    col_send(0)
    event(3, 3)
    row_send(2)
    col_send(1)
    arrived(3, 3)
    project(3)

    for h in range(2):
        hr = slice(h * rows, (h + 1) * rows)
        rounded = dA[:, h * hd : (h + 1) * hd].astype(BF).astype(F32)
        scaled = (rounded * rl[hr, :]).astype(BF)
        dAs[hr, :] = scaled
        wide = scaled.astype(F32)
        dAsT[:, hr] = wide.T.astype(BF)
        d = jnp.sum(wide * att2[hr, :].astype(F32), axis=1, keepdims=True)
        delta[hr, :] = jnp.broadcast_to(d, (rows, hd))

    odd(4, True)
    odd(3)
    backward(6, ebuf.at[3])
    send_back(3)
    weight_grad(3)
    odd(2)
    backward(4, ebuf.at[2])
    send_back(2)
    odd(1)
    col_send(2)
    row_send(3)
    backward(8, ebuf.at[4])
    backward(2, ebuf.at[1])
    send_back(1)
    backward(0, ebuf.at[0])
    for h in range(2):
        hr = slice(h * rows, (h + 1) * rows)
        dq_o[:, h * hd : (h + 1) * hd] = (dq[hr, :] * SCALE).astype(BF)

    @pl.when(core == 1)
    def _():
        sib_copy(4).wait_recv()

    for h in (0, 1):
        hr = pl.ds(h * hd, hd)
        total = ebuf[4, hr, :] + jnp.where(core == 1, srecv[4, hr, :].astype(F32), 0.0)
        for i in (3, 2):
            back_copy(i, h).wait_recv()
            total = total + jnp.where(y + i >= SIDE, rrecv[i, hr, :].astype(F32), 0.0)
        lsend[hr, :] = total.astype(BF)
        relay(h).start()
    col_send(3)
    own = xown[...]
    for i in (1, 2, 3):
        col_from(i).wait_recv()
        own = own + xrecv[i].astype(F32)
    dwo_o[...] = own

    @pl.when(core == 0)
    def _():
        sib_copy(1).wait_recv()

    for h in (0, 1):
        hr = pl.ds(h * hd, hd)
        total = ebuf[0, hr, :] + jnp.where(core == 0, srecv[1, hr, :].astype(F32), 0.0)
        for i in (3, 2):
            total = total + jnp.where(y + i < SIDE, rrecv[i, hr, :].astype(F32), 0.0)
        back_copy(1, h).wait_recv()
        total = total + rrecv[1, hr, :].astype(F32)
        relay(h).wait_recv()
        total = total + lrecv[hr, :].astype(F32)
        if h == 0:
            dk_o[...] = (total.T * SCALE).astype(BF)
        else:
            dv_o[...] = total.T.astype(BF)

    for f in range(slices):
        for way in (0, 1):
            for kind in range(4):
                ring_copy(way, kind, f, kind).wait_send()
        pair_copy(f).wait_send()
        for i in (1, 2, 3):
            row_copy(f, i).wait_send()

        @pl.when(x != f)
        def _():
            col_copy(f).wait_send()
    hx().wait_send()
    for i in (1, 2, 3):
        hy(i, 0).wait_send()
        for h in (0, 1):
            back_copy(i, h).wait_send()
    for j in (1, 2, 3, 4):
        hs_from(j).wait_send()
        sib_copy(j).wait_send()
    for h in (0, 1):
        relay(h).wait_send()


def finish(*refs):
    count = len(refs) // 2
    for given, laid in zip(refs[:count], refs[count:]):
        laid[...] = given[...].reshape(laid.shape)


def per_device(queries, keys, values, out_weight, cotangent, advantages, lengths):
    rows, heads, hd = queries.shape
    width = heads * hd
    depth = cotangent.shape[1]
    slices = SIDE
    fs = depth // slices
    own = depth // lax.axis_size("seq")
    q_rows = heads * rows
    vmem = pl.BlockSpec(memory_space=pltpu.VMEM)
    anywhere = pl.BlockSpec(memory_space=pl.ANY)
    smem = pl.BlockSpec(memory_space=pltpu.SMEM)
    dma = pltpu.SemaphoreType.DMA
    V = pltpu.VMEM
    out = pl.pallas_call(
        kernel,
        out_shape=[
            jax.ShapeDtypeStruct((rows, width), BF),
            jax.ShapeDtypeStruct((rows, width), BF),
            jax.ShapeDtypeStruct((rows, hd), BF),
            jax.ShapeDtypeStruct((rows, hd), BF),
            jax.ShapeDtypeStruct((own, width), F32),
        ],
        in_specs=[smem, smem, vmem, vmem, vmem, anywhere, vmem],
        out_specs=[vmem] * 5,
        scratch_shapes=[
            V((slices, rows, fs), BF),
            V((width, depth), BF),
            V((BACK + 1, rows, 2 * hd), BF),
            V((q_rows, hd), BF),
            V((hd, q_rows), BF),
            V((rows, hd), jnp.int32),
            V((BACK + 1, q_rows, rows), F32),
            V((BACK + 1, q_rows, rows), BF),
            V((q_rows, hd), F32),
            V((q_rows, hd), F32),
            V((q_rows, hd), F32),
            V((q_rows, hd), BF),
            V((rows, width), F32),
            V((q_rows, hd), BF),
            V((hd, q_rows), BF),
            V((q_rows, hd), F32),
            V((q_rows, hd), F32),
            V((q_rows, rows), BF),
            V((slices, SIDE, own, width), BF),
            V((slices, SIDE, own, width), BF),
            V((slices, SIDE, own, width), BF),
            V((slices, SIDE, own, width), BF),
            V((slices, own, width), F32),
            V((slices, own, width), BF),
            V((SIDE, own, width), BF),
            V((own, width), F32),
            V((5, 2 * hd, rows), BF),
            V((5, 2 * hd, rows), BF),
            V((4, 2 * hd, rows), BF),
            V((4, 2 * hd, rows), BF),
            V((2 * hd, rows), BF),
            V((2 * hd, rows), BF),
            dma((2, 4, slices)),
            dma((2, 4, slices)),
            dma,
            dma((2,)),
            dma((2, 4)),
            dma((2, 5)),
            dma((2, slices)),
            dma((2, slices, 4)),
            dma((slices,)),
            dma((4,)),
            dma((2, 5)),
            dma((2, 4, 2)),
            dma((2, 2)),
        ],
        compiler_params=pltpu.CompilerParams(
            collective_id=0, has_side_effects=True, vmem_limit_bytes=60 * 1024 * 1024
        ),
        cost_estimate=pl.CostEstimate(flops=9 * 10**9, bytes_accessed=5 * 10**6, transcendentals=5 * 10**6),
        name="rollout_attention",
    )(lengths, advantages, queries, keys.reshape(rows, hd), values.reshape(rows, hd), out_weight, cotangent)
    attention, d_queries, d_keys, d_values, d_weight = pl.pallas_call(
        finish,
        out_shape=[
            jax.ShapeDtypeStruct((rows, heads, hd), BF),
            jax.ShapeDtypeStruct((rows, heads, hd), BF),
            jax.ShapeDtypeStruct((rows, hd), BF),
            jax.ShapeDtypeStruct((rows, hd), BF),
            jax.ShapeDtypeStruct((own, width), F32),
        ],
        in_specs=[vmem] * 5,
        out_specs=[vmem] * 5,
        name="lay_out_results",
    )(*out)
    return (attention, d_queries, d_keys.reshape(rows, 1, hd), d_values.reshape(rows, 1, hd), d_weight)


def solution(mesh):
    tokens = P("seq", "tp", None)
    return jax.shard_map(
        per_device,
        mesh=mesh,
        in_specs=(tokens, tokens, tokens, P("tp", None), P(("seq", "tp"), None), P(), P()),
        out_specs=(tokens, tokens, tokens, tokens, P("seq", "tp")),
        check_vma=False,
    )
```

```python
import functools
import math

import jax
import jax.numpy as jnp
from jax import lax
from jax.experimental import pallas as pl
from jax.experimental.pallas import tpu as pltpu
from jax.sharding import PartitionSpec as P

WINDOW = 4096
SIDE = 4
RING = 8
BACK = 8
SCALE = 1.0 / 12.0
EXP2_SCALE = SCALE * math.log2(math.e)
MASKED = -1e30
BF = jnp.bfloat16
F32 = jnp.float32
MESH = pl.DeviceIdType.MESH
NN = (((1,), (0,)), ((), ()))
NT = (((1,), (1,)), ((), ()))
TN = (((0,), (0,)), ((), ()))


def dot(a, b, dims):
    return lax.dot_general(a, b, dims, preferred_element_type=F32)


def kernel(
    lens, adv, q_ref, k_ref, v_ref, w_hbm, cot_ref,
    att_o, dq_o, dk_o, dv_o, dwo_o,
    att, sc, w, kv, q2, qT, lo, hi, S, Pb, mx, rl, O2, att2,
    dA, dAs, dAsT, delta, dq, dS,
    psend, precv, ysend, yrecv, yown, xsend, xrecv, xown,
    ssend, srecv, rsend, rrecv, lsend, lrecv,
    gs_sem, gr_sem, w_sem, hx_sem, hy_sem, hs_sem,
    pp_sem, yy_sem, xs_sem, xr_sem, ss_sem, rr_sem, ll_sem,
):
    s = lax.axis_index("seq")
    z = lax.axis_index("tp")
    core = lax.rem(s, 2)
    chip = s // 2
    y = lax.rem(chip, SIDE)
    x = chip // SIDE
    rows, fs = sc.shape[1], sc.shape[2]
    ebuf = S.at[:, pl.ds(fs // 2, 2 * k_ref.shape[1]), :]
    slices = sc.shape[0]
    part = rows // RING
    hd = k_ref.shape[1]
    own_rows = dwo_o.shape[0]

    def row_dev(i):
        return {"seq": x * (2 * SIDE) + lax.rem(y + i + SIDE, SIDE) * 2 + core}

    def col_dev(i):
        return {"seq": lax.rem(x + i + SIDE, SIDE) * (2 * SIDE) + y * 2 + core}

    def ring_dev(i):
        return {"tp": lax.rem(z + i + RING, RING)}

    sib_dev = {"seq": s + 1 - 2 * core}

    def remote(src, dst, send, recv, dev):
        return pltpu.make_async_remote_copy(
            src_ref=src, dst_ref=dst, send_sem=send, recv_sem=recv, device_id=dev, device_id_type=MESH
        )

    barrier = pltpu.get_barrier_semaphore()
    next_dev = {"seq": lax.rem(s + 2, 2 * SIDE * SIDE)}
    last_dev = {"seq": lax.rem(s - 2 + 2 * SIDE * SIDE, 2 * SIDE * SIDE)}
    around = [f(i) for f in (row_dev, col_dev) for i in (1, 2, 3)]
    for dev in [sib_dev, ring_dev(1), ring_dev(-1), next_dev] + around:
        pl.semaphore_signal(barrier, inc=1, device_id=dev, device_id_type=MESH)
    w_copy = pltpu.make_async_copy(w_hbm, w, w_sem)
    w_copy.start()

    place = s * rows + z * part + lax.broadcasted_iota(jnp.int32, (part, hd), 0)
    factor = jnp.full((part, hd), adv[0], F32)
    cum = jnp.int32(0)
    for r in range(lens.shape[0] - 1):
        cum = cum + lens[r]
        factor = jnp.where(place >= cum, adv[r + 1], factor)
    wide = jnp.concatenate([factor] * (fs // hd), axis=1)
    my_rows = pl.ds(0, part)
    for f in range(slices):
        piece = cot_ref[:, f * fs : (f + 1) * fs].astype(F32)
        sc[f, my_rows, :] = (wide * piece).astype(BF)
    kv[0, :, :hd] = k_ref[...]
    kv[0, :, hd:] = v_ref[...]

    pl.semaphore_wait(barrier, 10)

    offsets = (0, 1, -1, 2, -2, 3, -3, 4)

    def chunk_of(p):
        return pl.ds(pl.multiple_of(lax.rem(z + offsets[p] + RING, RING) * part, part), part)

    def spot(away, kind, way):
        p = offsets.index(away if abs(away) < 4 else 4)
        if kind < 3:
            return pl.ds(p * part, part)
        return pl.ds(p * part + way * (part // 2), part // 2)

    def ring_copy(way, kind, f):
        sign = 1 - 2 * way
        src = sc.at[f, spot(-sign * kind, kind, way)]
        dst = sc.at[f, spot(-sign * (kind + 1), kind, way)]
        return remote(src, dst, gs_sem.at[way, kind, f], gr_sem.at[way, kind, f], ring_dev(sign))

    def arrived(kind, f):
        for way in (0, 1):
            ring_copy(way, kind, f).wait_recv()

    def event(kind, f):
        if kind:
            arrived(kind - 1, f)
        for way in (0, 1):
            ring_copy(way, kind, f).start()

    event(0, 0)
    event(0, 1)

    def hx():
        return remote(kv.at[0], kv.at[8], hx_sem.at[0], hx_sem.at[1], col_dev(1))

    hx().start()

    def hy(i, slot):
        return remote(kv.at[slot], kv.at[2 * i], hy_sem.at[0, i], hy_sem.at[1, i], row_dev(i))

    def hs(i):
        j = i + 1 - core
        return remote(kv.at[2 * i], kv.at[2 * j - 1], hs_sem.at[0, j], hs_sem.at[1, j], sib_dev)

    def hs_from(j):
        return remote(kv.at[2 * j], kv.at[2 * j - 1], hs_sem.at[0, j], hs_sem.at[1, j], sib_dev)

    for i in (1, 2, 3):
        @pl.when(y + i < SIDE)
        def _():
            hy(i, 0).start()

    @pl.when(core == 0)
    def _():
        hs(0).start()

    for p in range(RING):
        here = pl.ds(p * part, part)
        for h in range(2):
            q2[h * rows + p * part : h * rows + (p + 1) * part, :] = q_ref[chunk_of(p), h, :]
        local = lax.rem(z + offsets[p] + RING, RING) * part + lax.broadcasted_iota(jnp.int32, (part, hd), 0)
        place = s * rows + local
        first = jnp.zeros((part, hd), jnp.int32)
        cum = jnp.int32(0)
        for r in range(lens.shape[0] - 1):
            cum = cum + lens[r]
            first = jnp.where(place >= cum, cum, first)
        lo[here, :] = jnp.maximum(first, place - (WINDOW - 1)) - s * rows
        hi[here, :] = local
    qT[...] = q2[...].astype(F32).T.astype(BF)

    tile = 256
    tiles = 2 * rows // tile
    per_head = rows // tile

    def tile_rows(r):
        return pl.ds(pl.multiple_of(r * tile, tile), tile)

    def scores(d):
        def step(r, carry):
            at = tile_rows(r)
            raw = dot(q2[at, :], kv[d, :, :hd], NT)
            t0 = lax.rem(r, per_head) * tile
            low = lo[pl.ds(pl.multiple_of(t0, tile), tile), :] + d * rows
            best = None
            for c in range(rows // hd):
                col = lax.broadcasted_iota(jnp.int32, (tile, hd), 1) + c * hd
                seen = col >= low
                if d == 0:
                    seen = seen & (col <= hi[pl.ds(pl.multiple_of(t0, tile), tile), :])
                val = jnp.where(seen, raw[:, c * hd : (c + 1) * hd], MASKED)
                S[d, at, c * hd : (c + 1) * hd] = val
                best = val if best is None else jnp.maximum(best, val)
            mx[at, :] = best if d == 0 else jnp.maximum(mx[at, :], best)
            return carry

        lax.fori_loop(0, tiles, step, 0)

    def weigh(r, last):
        at = pl.ds(r * tile, tile)
        if not last:
            mx[at, :] = jnp.broadcast_to(jnp.max(mx[at, :], axis=1, keepdims=True), (tile, hd))
            rl[at, :] = jnp.zeros((tile, hd), F32)
            O2[at, :] = jnp.zeros((tile, hd), F32)

        def step(d, carry):
            top = mx[at, :]
            total = rl[at, :]
            for c in range(rows // hd):
                p = jnp.exp2((S[d, at, c * hd : (c + 1) * hd] - top) * EXP2_SCALE)
                total = total + p
                Pb[d, at, c * hd : (c + 1) * hd] = p.astype(BF)
            rl[at, :] = total
            O2[at, :] += dot(Pb[d, at, :], kv[d, :, hd:], NN)
            return carry

        middle = BACK // 2
        if not last:
            lax.fori_loop(0, middle, step, 0)
            return
        lax.fori_loop(middle, BACK + 1, step, 0)
        inv = 1.0 / jnp.broadcast_to(jnp.sum(rl[at, :], axis=1, keepdims=True), (tile, hd))
        rl[at, :] = inv
        out = (O2[at, :] * inv).astype(BF)
        att2[at, :] = out
        t0, h = (r % per_head) * tile, r // per_head
        att[t0 : t0 + tile, h * hd : (h + 1) * hd] = out
        for p in range(t0 // part, (t0 + tile) // part):
            att_o[chunk_of(p), h * hd : (h + 1) * hd] = out[p * part - t0 : (p + 1) * part - t0]

    def project(f, g=None):
        at = pl.ds(0, rows) if g is None else pl.ds(g * tile, tile)
        term = dot(sc[f, at, :], w[:, f * fs : (f + 1) * fs], NT)
        if f == 0:
            dA[at, :] = term
        else:
            dA[at, :] += term

    def pair_copy(f):
        return remote(psend.at[f], precv.at[f], pp_sem.at[0, f], pp_sem.at[1, f], sib_dev)

    def weight_rows(f, j, which):
        width = att.shape[1]
        at = pl.ds(pl.multiple_of((2 * (j % 2) + which) * own_rows, own_rows), own_rows)
        return S[BACK - f, at, (j // 2) * width : (j // 2 + 1) * width]

    def weight_grad(f):
        width = att.shape[1]
        cut = fs // 2
        for i in range(fs // hd):
            term = dot(sc[f, :, i * hd : (i + 1) * hd], att[...], TN)
            for side in (0, 1):
                first, last = max(i * hd, side * cut), min((i + 1) * hd, (side + 1) * cut)
                if first < last:
                    S[BACK - f, first - side * cut : last - side * cut, pl.ds(side * width, width)] = (
                        term[first - i * hd : last - i * hd]
                    )
        for j in range(SIDE):
            psend[f, j] = weight_rows(f, j, 1 - core).astype(BF)
        pair_copy(f).start()

    def row_copy(f, i):
        return remote(ysend.at[f, i], yrecv.at[f, i], yy_sem.at[0, f, i], yy_sem.at[1, f, i], row_dev(i))

    def row_send(f):
        pair_copy(f).wait_recv()
        for j in range(SIDE):
            both = weight_rows(f, j, core) + precv[f, j].astype(F32)
            ysend[f, lax.rem(j - y + SIDE, SIDE)] = both.astype(BF)

            @pl.when(y == j)
            def _():
                yown[f] = both

        for i in (1, 2, 3):
            row_copy(f, i).start()

    def col_copy(f):
        slot = lax.rem(x - f + SIDE, SIDE)
        return remote(
            xsend.at[f], xrecv.at[slot], xs_sem.at[f], xr_sem.at[slot],
            {"seq": f * (2 * SIDE) + y * 2 + core},
        )

    def col_from(i):
        return remote(xsend.at[i], xrecv.at[i], xs_sem.at[i], xr_sem.at[i], col_dev(i))

    def col_send(f):
        total = yown[f]
        for i in (1, 2, 3):
            row_copy(f, i).wait_recv()
            total = total + yrecv[f, i].astype(F32)

        @pl.when(x == f)
        def _():
            xown[...] = total

        @pl.when(x != f)
        def _():
            xsend[f] = total.astype(BF)
            col_copy(f).start()

    def ready(g):
        for h in range(2):
            at = pl.ds(h * rows + g * tile, tile)
            rounded = dA[pl.ds(g * tile, tile), h * hd : (h + 1) * hd].astype(BF).astype(F32)
            scaled = (rounded * rl[at, :]).astype(BF)
            dAs[at, :] = scaled
            wide = scaled.astype(F32)
            dAsT[:, at] = wide.T.astype(BF)
            d = jnp.sum(wide * att2[at, :].astype(F32), axis=1, keepdims=True)
            delta[at, :] = jnp.broadcast_to(d, (tile, hd))

    def backward(d, g, out, first=False):
        dk_part, dv_part = 0.0, 0.0
        for h in range(2):
            at = pl.ds(h * rows + g * tile, tile)
            raw = dot(dAs[at, :], kv[d, :, hd:], NT)
            low = delta[at, :]
            for c in range(rows // hd):
                cs = slice(c * hd, (c + 1) * hd)
                dS[at, cs] = (Pb[d, at, cs].astype(F32) * (raw[:, cs] - low)).astype(BF)
            term = dot(dS[at, :], kv[d, :, :hd], NN)
            if first:
                dq[at, :] = term
            else:
                dq[at, :] += term
            dk_part += dot(qT[:, at], dS[at, :], NN)
            dv_part += dot(dAsT[:, at], Pb[d, at, :], NN)
        if g:
            dk_part, dv_part = ebuf[d, :hd, :] + dk_part, ebuf[d, hd:, :] + dv_part
        out[:hd, :] = dk_part.astype(out.dtype)
        out[hd:, :] = dv_part.astype(out.dtype)

    def early(d, first=False):
        backward(d, 0, ebuf.at[d], first)

    def sib_copy(i):
        return remote(ssend.at[i], srecv.at[i], ss_sem.at[0, i], ss_sem.at[1, i], sib_dev)

    def half(ref, h):
        return ref.at[pl.ds(h * hd, hd)]

    def back_copy(i, h):
        dev = last_dev if i == 1 else row_dev(-i)
        return remote(half(rsend.at[i], h), half(rrecv.at[i], h), rr_sem.at[0, i, h], rr_sem.at[1, i, h], dev)

    def relay(h):
        return remote(half(lsend, h), half(lrecv, h), ll_sem.at[0, h], ll_sem.at[1, h], col_dev(-1))

    def odd(i, first=False):
        backward(2 * i - 1, 1, ssend.at[i], first)
        sib_copy(i).start()

    def send_back(i):
        j = i + 1 - core
        sib_copy(j).wait_recv()
        for h in (0, 1):
            hs_ = pl.ds(h * hd, hd)
            rsend[i, hs_, :] = (ebuf[2 * i, hs_, :] + srecv[j, hs_, :].astype(F32)).astype(BF)
            back_copy(i, h).start()

    def relay_in():
        hx().wait_recv()
        for i in (1, 2, 3):
            @pl.when(y + i >= SIDE)
            def _():
                hy(i, 8).start()

        @pl.when(core == 1)
        def _():
            hs(4).start()

    def even_in(i):
        hy(i, 0).wait_recv()
        hs(i).start()
        scores(2 * i)

    def odd_in(j):
        hs_from(j).wait_recv()
        scores(2 * j - 1)

    scores(0)
    event(1, 0)
    event(0, 2)
    relay_in()
    scores(8)
    event(1, 1)
    event(2, 0)
    even_in(1)
    event(2, 1)
    event(1, 2)
    odd_in(1)
    even_in(3)
    event(3, 0)
    event(0, 3)
    even_in(2)
    odd_in(2)
    odd_in(3)
    event(3, 1)
    odd_in(4)
    weigh(0, False)
    weigh(0, True)
    event(2, 2)
    weigh(1, False)
    weigh(1, True)
    w_copy.wait()
    arrived(3, 0)
    project(0)
    weigh(2, False)
    weigh(2, True)
    event(1, 3)
    weigh(3, False)
    arrived(3, 1)
    project(1)
    weigh(3, True)
    weight_grad(0)
    event(3, 2)
    project(2, 0)
    weight_grad(1)
    row_send(0)
    event(2, 3)
    project(3, 0)
    ready(0)
    early(7, True)
    row_send(1)
    early(5)
    early(6)
    arrived(3, 2)
    project(2, 1)
    event(3, 3)
    weight_grad(2)
    early(3)
    early(4)
    row_send(2)
    early(1)
    col_send(0)
    early(8)
    early(2)
    early(0)
    arrived(3, 3)
    project(3, 1)
    ready(1)
    odd(4, True)
    weight_grad(3)
    odd(3)
    backward(6, 1, ebuf.at[6])
    send_back(3)
    row_send(3)
    odd(2)
    backward(4, 1, ebuf.at[4])
    send_back(2)
    odd(1)
    backward(2, 1, ebuf.at[2])
    send_back(1)
    backward(8, 1, ebuf.at[8])
    backward(0, 1, ebuf.at[0])
    col_send(1)
    col_send(2)
    for p in range(RING):
        for h in range(2):
            grad = dq[pl.ds(h * rows + p * part, part), :] * SCALE
            dq_o[chunk_of(p), h * hd : (h + 1) * hd] = grad.astype(BF)

    @pl.when(core == 1)
    def _():
        sib_copy(4).wait_recv()

    for h in (0, 1):
        hr = pl.ds(h * hd, hd)
        total = ebuf[8, hr, :] + jnp.where(core == 1, srecv[4, hr, :].astype(F32), 0.0)
        for i in (3, 2):
            back_copy(i, h).wait_recv()
            total = total + jnp.where(y + i >= SIDE, rrecv[i, hr, :].astype(F32), 0.0)
        lsend[hr, :] = total.astype(BF)
        relay(h).start()
    col_send(3)
    own = xown[...]
    for i in (1, 2, 3):
        col_from(i).wait_recv()
        own = own + xrecv[i].astype(F32)
    dwo_o[...] = own

    @pl.when(core == 0)
    def _():
        sib_copy(1).wait_recv()

    for h in (0, 1):
        hr = pl.ds(h * hd, hd)
        total = ebuf[0, hr, :] + jnp.where(core == 0, srecv[1, hr, :].astype(F32), 0.0)
        for i in (3, 2):
            total = total + jnp.where(y + i < SIDE, rrecv[i, hr, :].astype(F32), 0.0)
        back_copy(1, h).wait_recv()
        total = total + rrecv[1, hr, :].astype(F32)
        relay(h).wait_recv()
        total = total + lrecv[hr, :].astype(F32)
        if h == 0:
            dk_o[...] = (total.T * SCALE).astype(BF)
        else:
            dv_o[...] = total.T.astype(BF)

    for f in range(slices):
        for way in (0, 1):
            for kind in range(4):
                ring_copy(way, kind, f).wait_send()
        pair_copy(f).wait_send()
        for i in (1, 2, 3):
            row_copy(f, i).wait_send()

        @pl.when(x != f)
        def _():
            col_copy(f).wait_send()
    hx().wait_send()
    for i in (1, 2, 3):
        hy(i, 0).wait_send()
        for h in (0, 1):
            back_copy(i, h).wait_send()
    for j in (1, 2, 3, 4):
        hs_from(j).wait_send()
        sib_copy(j).wait_send()
    for h in (0, 1):
        relay(h).wait_send()


def finish(*refs):
    count = len(refs) // 2
    for given, laid in zip(refs[:count], refs[count:]):
        laid[...] = given[...].reshape(laid.shape)


def per_device(queries, keys, values, out_weight, cotangent, advantages, lengths):
    rows, heads, hd = queries.shape
    width = heads * hd
    depth = cotangent.shape[1]
    slices = SIDE
    fs = depth // slices
    own = depth // lax.axis_size("seq")
    q_rows = heads * rows
    vmem = pl.BlockSpec(memory_space=pltpu.VMEM)
    anywhere = pl.BlockSpec(memory_space=pl.ANY)
    smem = pl.BlockSpec(memory_space=pltpu.SMEM)
    dma = pltpu.SemaphoreType.DMA
    V = pltpu.VMEM
    out = pl.pallas_call(
        kernel,
        out_shape=[
            jax.ShapeDtypeStruct((rows, width), BF),
            jax.ShapeDtypeStruct((rows, width), BF),
            jax.ShapeDtypeStruct((rows, hd), BF),
            jax.ShapeDtypeStruct((rows, hd), BF),
            jax.ShapeDtypeStruct((own, width), F32),
        ],
        in_specs=[smem, smem, vmem, vmem, vmem, anywhere, vmem],
        out_specs=[vmem] * 5,
        scratch_shapes=[
            V((rows, width), BF),
            V((slices, rows, fs), BF),
            V((width, depth), BF),
            V((BACK + 1, rows, 2 * hd), BF),
            V((q_rows, hd), BF),
            V((hd, q_rows), BF),
            V((rows, hd), jnp.int32),
            V((rows, hd), jnp.int32),
            V((BACK + 1, q_rows, rows), F32),
            V((BACK + 1, q_rows, rows), BF),
            V((q_rows, hd), F32),
            V((q_rows, hd), F32),
            V((q_rows, hd), F32),
            V((q_rows, hd), BF),
            V((rows, width), F32),
            V((q_rows, hd), BF),
            V((hd, q_rows), BF),
            V((q_rows, hd), F32),
            V((q_rows, hd), F32),
            V((q_rows, rows), BF),
            V((slices, SIDE, own, width), BF),
            V((slices, SIDE, own, width), BF),
            V((slices, SIDE, own, width), BF),
            V((slices, SIDE, own, width), BF),
            V((slices, own, width), F32),
            V((slices, own, width), BF),
            V((SIDE, own, width), BF),
            V((own, width), F32),
            V((5, 2 * hd, rows), BF),
            V((5, 2 * hd, rows), BF),
            V((4, 2 * hd, rows), BF),
            V((4, 2 * hd, rows), BF),
            V((2 * hd, rows), BF),
            V((2 * hd, rows), BF),
            dma((2, 4, slices)),
            dma((2, 4, slices)),
            dma,
            dma((2,)),
            dma((2, 4)),
            dma((2, 5)),
            dma((2, slices)),
            dma((2, slices, 4)),
            dma((slices,)),
            dma((4,)),
            dma((2, 5)),
            dma((2, 4, 2)),
            dma((2, 2)),
        ],
        compiler_params=pltpu.CompilerParams(
            collective_id=0, has_side_effects=True, vmem_limit_bytes=60 * 1024 * 1024
        ),
        cost_estimate=pl.CostEstimate(flops=9 * 10**9, bytes_accessed=5 * 10**6, transcendentals=5 * 10**6),
        name="rollout_attention",
    )(lengths, advantages, queries, keys.reshape(rows, hd), values.reshape(rows, hd), out_weight, cotangent)
    attention, d_queries, d_keys, d_values, d_weight = pl.pallas_call(
        finish,
        out_shape=[
            jax.ShapeDtypeStruct((rows, heads, hd), BF),
            jax.ShapeDtypeStruct((rows, heads, hd), BF),
            jax.ShapeDtypeStruct((rows, hd), BF),
            jax.ShapeDtypeStruct((rows, hd), BF),
            jax.ShapeDtypeStruct((own, width), F32),
        ],
        in_specs=[vmem] * 5,
        out_specs=[vmem] * 5,
        name="lay_out_results",
    )(*out)
    return (attention, d_queries, d_keys.reshape(rows, 1, hd), d_values.reshape(rows, 1, hd), d_weight)


def solution(mesh):
    tokens = P("seq", "tp", None)
    return jax.shard_map(
        per_device,
        mesh=mesh,
        in_specs=(tokens, tokens, tokens, P("tp", None), P(("seq", "tp"), None), P(), P()),
        out_specs=(tokens, tokens, tokens, tokens, P("seq", "tp")),
        check_vma=False,
    )
```

```python
import functools
import math

import jax
import jax.numpy as jnp
from jax import lax
from jax.experimental import pallas as pl
from jax.experimental.pallas import tpu as pltpu
from jax.sharding import PartitionSpec as P

WINDOW = 4096
SIDE = 4
RING = 8
BACK = 8
SCALE = 1.0 / 12.0
EXP2_SCALE = SCALE * math.log2(math.e)
MASKED = -1e30
BF = jnp.bfloat16
F32 = jnp.float32
MESH = pl.DeviceIdType.MESH
NN = (((1,), (0,)), ((), ()))
NT = (((1,), (1,)), ((), ()))
TN = (((0,), (0,)), ((), ()))


def dot(a, b, dims):
    return lax.dot_general(a, b, dims, preferred_element_type=F32)


def kernel(
    lens, adv, q_hbm, k_hbm, v_hbm, w_hbm, cot_hbm,
    att_hbm, dq_hbm, dk_hbm, dv_hbm, dwo_hbm,
    q_ref, cot_ref, att_o, dq_o, dk_o, dv_o, dwo_o,
    sc, w, kv, q2, qT, lo, S, Pb, mx, rl, O2, att2,
    dA, dAs, dAsT, delta, dq, dS,
    psend, precv, ysend, yrecv, yown, xsend, xrecv, xown,
    ssend, srecv, rsend, rrecv, lsend, lrecv,
    gs_sem, gr_sem, w_sem, hx_sem, hy_sem, hs_sem,
    pp_sem, yy_sem, xs_sem, xr_sem, ss_sem, rr_sem, ll_sem, in_sem, out_sem,
):
    s = lax.axis_index("seq")
    z = lax.axis_index("tp")
    core = lax.rem(s, 2)
    chip = s // 2
    y = lax.rem(chip, SIDE)
    x = chip // SIDE
    rows, fs = sc.shape[1], sc.shape[2]
    ebuf = S.at[:, : 2 * k_hbm.shape[1], :]
    slices = sc.shape[0]
    part = rows // RING
    hd = k_hbm.shape[1]
    own_rows = dwo_o.shape[0]

    def row_dev(i):
        return {"seq": x * (2 * SIDE) + lax.rem(y + i + SIDE, SIDE) * 2 + core}

    def col_dev(i):
        return {"seq": lax.rem(x + i + SIDE, SIDE) * (2 * SIDE) + y * 2 + core}

    def ring_dev(i):
        return {"tp": lax.rem(z + i + RING, RING)}

    sib_dev = {"seq": s + 1 - 2 * core}

    def remote(src, dst, send, recv, dev):
        return pltpu.make_async_remote_copy(
            src_ref=src, dst_ref=dst, send_sem=send, recv_sem=recv, device_id=dev, device_id_type=MESH
        )

    barrier = pltpu.get_barrier_semaphore()
    next_dev = {"seq": lax.rem(s + 2, 2 * SIDE * SIDE)}
    last_dev = {"seq": lax.rem(s - 2 + 2 * SIDE * SIDE, 2 * SIDE * SIDE)}
    around = [f(i) for f in (row_dev, col_dev) for i in (1, 2, 3)]
    for dev in [sib_dev, ring_dev(1), ring_dev(-1), next_dev] + around:
        pl.semaphore_signal(barrier, inc=1, device_id=dev, device_id_type=MESH)
    w_copy = pltpu.make_async_copy(w_hbm, w, w_sem)
    cot_in = pltpu.make_async_copy(cot_hbm, cot_ref, in_sem.at[0])
    k_in = pltpu.make_async_copy(k_hbm, kv.at[0, :, pl.ds(0, hd)], in_sem.at[1])
    v_in = pltpu.make_async_copy(v_hbm, kv.at[0, :, pl.ds(hd, hd)], in_sem.at[2])
    q_in = pltpu.make_async_copy(q_hbm, q_ref, in_sem.at[3])
    for copy in (cot_in, k_in, v_in, q_in, w_copy):
        copy.start()
    leaving = [
        pltpu.make_async_copy(ref, out, out_sem.at[i])
        for i, (ref, out) in enumerate(
            ((att_o, att_hbm), (dq_o, dq_hbm), (dk_o, dk_hbm), (dv_o, dv_hbm), (dwo_o, dwo_hbm))
        )
    ]

    place = s * rows + z * part + lax.broadcasted_iota(jnp.int32, (part, hd), 0)
    factor = jnp.full((part, hd), adv[0], F32)
    cum = jnp.int32(0)
    for r in range(lens.shape[0] - 1):
        cum = cum + lens[r]
        factor = jnp.where(place >= cum, adv[r + 1], factor)
    wide = jnp.concatenate([factor] * (fs // hd), axis=1)
    my_rows = pl.ds(pl.multiple_of(z * part, part), part)
    cot_in.wait()
    for f in range(slices):
        piece = cot_ref[:, f * fs : (f + 1) * fs].astype(F32)
        sc[f, my_rows, :] = (wide * piece).astype(BF)

    pl.semaphore_wait(barrier, 10)

    def chunk_rows(sign, away, kind):
        chunk = lax.rem(z - sign * away + RING, RING)
        half = part // 2
        if kind < 3:
            return pl.ds(pl.multiple_of(chunk * part, part), part)
        return pl.ds(pl.multiple_of(chunk * part + (0 if sign > 0 else half), half), half)

    def ring_copy(way, kind, f, away):
        sign = 1 - 2 * way
        ref = sc.at[f, chunk_rows(sign, away, kind)]
        return remote(ref, ref, gs_sem.at[way, kind, f], gr_sem.at[way, kind, f], ring_dev(sign))

    def arrived(kind, f):
        for way in (0, 1):
            ring_copy(way, kind, f, kind + 1).wait_recv()

    def event(kind, f):
        if kind:
            arrived(kind - 1, f)
        for way in (0, 1):
            ring_copy(way, kind, f, kind).start()

    event(0, 0)
    event(0, 1)

    k_in.wait()
    v_in.wait()

    def hx():
        return remote(kv.at[0], kv.at[8], hx_sem.at[0], hx_sem.at[1], col_dev(1))

    hx().start()

    def hy(i, slot):
        return remote(kv.at[slot], kv.at[2 * i], hy_sem.at[0, i], hy_sem.at[1, i], row_dev(i))

    def hs(i):
        j = i + 1 - core
        return remote(kv.at[2 * i], kv.at[2 * j - 1], hs_sem.at[0, j], hs_sem.at[1, j], sib_dev)

    def hs_from(j):
        return remote(kv.at[2 * j], kv.at[2 * j - 1], hs_sem.at[0, j], hs_sem.at[1, j], sib_dev)

    for i in (1, 2, 3):
        @pl.when(y + i < SIDE)
        def _():
            hy(i, 0).start()

    @pl.when(core == 0)
    def _():
        hs(0).start()

    q_in.wait()
    q2[:rows, :] = q_ref[:, 0, :]
    q2[rows:, :] = q_ref[:, 1, :]
    qT[...] = q2[...].astype(F32).T.astype(BF)
    place = s * rows + lax.broadcasted_iota(jnp.int32, (rows, hd), 0)
    first = jnp.zeros((rows, hd), jnp.int32)
    cum = jnp.int32(0)
    for r in range(lens.shape[0] - 1):
        cum = cum + lens[r]
        first = jnp.where(place >= cum, cum, first)
    lo[...] = jnp.maximum(first, place - (WINDOW - 1)) - s * rows

    tile = 256
    tiles = 2 * rows // tile
    per_head = rows // tile

    def tile_rows(r):
        return pl.ds(pl.multiple_of(r * tile, tile), tile)

    def scores(d):
        def step(r, carry):
            at = tile_rows(r)
            raw = dot(q2[at, :], kv[d, :, :hd], NT)
            t0 = lax.rem(r, per_head) * tile
            low = lo[pl.ds(pl.multiple_of(t0, tile), tile), :] + d * rows
            best = None
            for c in range(rows // hd):
                col = lax.broadcasted_iota(jnp.int32, (tile, hd), 1) + c * hd
                seen = col >= low
                if d == 0:
                    seen = seen & (col <= lax.broadcasted_iota(jnp.int32, (tile, hd), 0) + t0)
                val = jnp.where(seen, raw[:, c * hd : (c + 1) * hd], MASKED)
                S[d, at, c * hd : (c + 1) * hd] = val
                best = val if best is None else jnp.maximum(best, val)
            mx[at, :] = best if d == 0 else jnp.maximum(mx[at, :], best)
            return carry

        lax.fori_loop(0, tiles, step, 0)

    def weigh(r, last):
        at = pl.ds(r * tile, tile)
        if not last:
            mx[at, :] = jnp.broadcast_to(jnp.max(mx[at, :], axis=1, keepdims=True), (tile, hd))
            rl[at, :] = jnp.zeros((tile, hd), F32)
            O2[at, :] = jnp.zeros((tile, hd), F32)

        def step(d, carry):
            top = mx[at, :]
            total = rl[at, :]
            for c in range(rows // hd):
                p = jnp.exp2((S[d, at, c * hd : (c + 1) * hd] - top) * EXP2_SCALE)
                total = total + p
                Pb[d, at, c * hd : (c + 1) * hd] = p.astype(BF)
            rl[at, :] = total
            O2[at, :] += dot(Pb[d, at, :], kv[d, :, hd:], NN)
            return carry

        middle = BACK // 2
        if not last:
            lax.fori_loop(0, middle, step, 0)
            return
        lax.fori_loop(middle, BACK + 1, step, 0)
        inv = 1.0 / jnp.broadcast_to(jnp.sum(rl[at, :], axis=1, keepdims=True), (tile, hd))
        rl[at, :] = inv
        out = (O2[at, :] * inv).astype(BF)
        att2[at, :] = out
        t0, h = (r % per_head) * tile, r // per_head
        att_o[t0 : t0 + tile, h * hd : (h + 1) * hd] = out

    def project(f):
        term = dot(sc[f], w[:, f * fs : (f + 1) * fs], NT)
        if f == 0:
            dA[...] = term
        else:
            dA[...] += term

    def pair_copy(f):
        return remote(psend.at[f], precv.at[f], pp_sem.at[0, f], pp_sem.at[1, f], sib_dev)

    def weight_rows(f, j, which):
        width = att_o.shape[1]
        at = pl.ds(pl.multiple_of((2 * (j % 2) + which) * own_rows, own_rows), own_rows)
        return S[BACK - f, at, (j // 2) * width : (j // 2 + 1) * width]

    def weight_grad(f):
        width = att_o.shape[1]
        cut = fs // 2
        for i in range(fs // hd):
            term = dot(sc[f, :, i * hd : (i + 1) * hd], att_o[...], TN)
            for side in (0, 1):
                first, last = max(i * hd, side * cut), min((i + 1) * hd, (side + 1) * cut)
                if first < last:
                    S[BACK - f, first - side * cut : last - side * cut, pl.ds(side * width, width)] = (
                        term[first - i * hd : last - i * hd]
                    )
        for j in range(SIDE):
            psend[f, j] = weight_rows(f, j, 1 - core).astype(BF)
        pair_copy(f).start()

    def row_copy(f, i):
        return remote(ysend.at[f, i], yrecv.at[f, i], yy_sem.at[0, f, i], yy_sem.at[1, f, i], row_dev(i))

    def row_send(f):
        pair_copy(f).wait_recv()
        for j in range(SIDE):
            both = weight_rows(f, j, core) + precv[f, j].astype(F32)
            ysend[f, lax.rem(j - y + SIDE, SIDE)] = both.astype(BF)

            @pl.when(y == j)
            def _():
                yown[f] = both

        for i in (1, 2, 3):
            row_copy(f, i).start()

    def col_copy(f):
        slot = lax.rem(x - f + SIDE, SIDE)
        return remote(
            xsend.at[f], xrecv.at[slot], xs_sem.at[f], xr_sem.at[slot],
            {"seq": f * (2 * SIDE) + y * 2 + core},
        )

    def col_from(i):
        return remote(xsend.at[i], xrecv.at[i], xs_sem.at[i], xr_sem.at[i], col_dev(i))

    def col_send(f):
        total = yown[f]
        for i in (1, 2, 3):
            row_copy(f, i).wait_recv()
            total = total + yrecv[f, i].astype(F32)

        @pl.when(x == f)
        def _():
            xown[...] = total

        @pl.when(x != f)
        def _():
            xsend[f] = total.astype(BF)
            col_copy(f).start()

    def backward(d, out, first=False):
        for r in range(tiles):
            at = pl.ds(r * tile, tile)
            raw = dot(dAs[at, :], kv[d, :, hd:], NT)
            low = delta[at, :]
            for c in range(rows // hd):
                cs = slice(c * hd, (c + 1) * hd)
                dS[at, cs] = (Pb[d, at, cs].astype(F32) * (raw[:, cs] - low)).astype(BF)
            term = dot(dS[at, :], kv[d, :, :hd], NN)
            if first:
                dq[at, :] = term
            else:
                dq[at, :] += term
        out[:hd, :] = dot(qT[...], dS[...], NN).astype(out.dtype)
        out[hd:, :] = dot(dAsT[...], Pb[d], NN).astype(out.dtype)

    def sib_copy(i):
        return remote(ssend.at[i], srecv.at[i], ss_sem.at[0, i], ss_sem.at[1, i], sib_dev)

    def half(ref, h):
        return ref.at[pl.ds(h * hd, hd)]

    def back_copy(i, h):
        dev = last_dev if i == 1 else row_dev(-i)
        return remote(half(rsend.at[i], h), half(rrecv.at[i], h), rr_sem.at[0, i, h], rr_sem.at[1, i, h], dev)

    def relay(h):
        return remote(half(lsend, h), half(lrecv, h), ll_sem.at[0, h], ll_sem.at[1, h], col_dev(-1))

    def odd(i, first=False):
        backward(2 * i - 1, ssend.at[i], first)
        sib_copy(i).start()

    def send_back(i):
        j = i + 1 - core
        sib_copy(j).wait_recv()
        for h in (0, 1):
            hs_ = pl.ds(h * hd, hd)
            rsend[i, hs_, :] = (ebuf[i, hs_, :] + srecv[j, hs_, :].astype(F32)).astype(BF)
            back_copy(i, h).start()

    def relay_in():
        hx().wait_recv()
        for i in (1, 2, 3):
            @pl.when(y + i >= SIDE)
            def _():
                hy(i, 8).start()

        @pl.when(core == 1)
        def _():
            hs(4).start()

    def even_in(i):
        hy(i, 0).wait_recv()
        hs(i).start()
        scores(2 * i)

    def odd_in(j):
        hs_from(j).wait_recv()
        scores(2 * j - 1)

    scores(0)
    event(1, 0)
    event(0, 2)
    relay_in()
    scores(8)
    event(1, 1)
    event(2, 0)
    even_in(1)
    event(2, 1)
    event(1, 2)
    odd_in(1)
    even_in(3)
    event(3, 0)
    event(0, 3)
    even_in(2)
    odd_in(2)
    odd_in(3)
    event(3, 1)
    odd_in(4)
    weigh(0, False)
    weigh(0, True)
    event(2, 2)
    weigh(1, False)
    weigh(1, True)
    w_copy.wait()
    arrived(3, 0)
    project(0)
    weigh(2, False)
    weigh(2, True)
    event(1, 3)
    weigh(3, False)
    arrived(3, 1)
    project(1)
    weigh(3, True)
    leaving[0].start()
    weight_grad(0)
    event(3, 2)

    weight_grad(1)
    row_send(0)
    event(2, 3)
    row_send(1)
    arrived(3, 2)
    project(2)
    weight_grad(2)
    col_send(0)
    event(3, 3)
    row_send(2)
    col_send(1)
    arrived(3, 3)
    project(3)

    for h in range(2):
        hr = slice(h * rows, (h + 1) * rows)
        rounded = dA[:, h * hd : (h + 1) * hd].astype(BF).astype(F32)
        scaled = (rounded * rl[hr, :]).astype(BF)
        dAs[hr, :] = scaled
        wide = scaled.astype(F32)
        dAsT[:, hr] = wide.T.astype(BF)
        d = jnp.sum(wide * att2[hr, :].astype(F32), axis=1, keepdims=True)
        delta[hr, :] = jnp.broadcast_to(d, (rows, hd))

    odd(4, True)
    odd(3)
    backward(6, ebuf.at[3])
    send_back(3)
    weight_grad(3)
    odd(2)
    backward(4, ebuf.at[2])
    send_back(2)
    odd(1)
    col_send(2)
    row_send(3)
    backward(8, ebuf.at[4])
    backward(2, ebuf.at[1])
    send_back(1)
    backward(0, ebuf.at[0])
    for h in range(2):
        hr = slice(h * rows, (h + 1) * rows)
        dq_o[:, h * hd : (h + 1) * hd] = (dq[hr, :] * SCALE).astype(BF)
    leaving[1].start()

    @pl.when(core == 1)
    def _():
        sib_copy(4).wait_recv()

    for h in (0, 1):
        hr = pl.ds(h * hd, hd)
        total = ebuf[4, hr, :] + jnp.where(core == 1, srecv[4, hr, :].astype(F32), 0.0)
        for i in (3, 2):
            back_copy(i, h).wait_recv()
            total = total + jnp.where(y + i >= SIDE, rrecv[i, hr, :].astype(F32), 0.0)
        lsend[hr, :] = total.astype(BF)
        relay(h).start()
    col_send(3)
    own = xown[...]
    for i in (1, 2, 3):
        col_from(i).wait_recv()
        own = own + xrecv[i].astype(F32)
    dwo_o[...] = own
    leaving[4].start()

    @pl.when(core == 0)
    def _():
        sib_copy(1).wait_recv()

    for h in (0, 1):
        hr = pl.ds(h * hd, hd)
        total = ebuf[0, hr, :] + jnp.where(core == 0, srecv[1, hr, :].astype(F32), 0.0)
        for i in (3, 2):
            total = total + jnp.where(y + i < SIDE, rrecv[i, hr, :].astype(F32), 0.0)
        back_copy(1, h).wait_recv()
        total = total + rrecv[1, hr, :].astype(F32)
        relay(h).wait_recv()
        total = total + lrecv[hr, :].astype(F32)
        if h == 0:
            dk_o[...] = (total.T * SCALE).astype(BF)
            leaving[2].start()
        else:
            dv_o[...] = total.T.astype(BF)
            leaving[3].start()

    for f in range(slices):
        for way in (0, 1):
            for kind in range(4):
                ring_copy(way, kind, f, kind).wait_send()
        pair_copy(f).wait_send()
        for i in (1, 2, 3):
            row_copy(f, i).wait_send()

        @pl.when(x != f)
        def _():
            col_copy(f).wait_send()
    hx().wait_send()
    for i in (1, 2, 3):
        hy(i, 0).wait_send()
        for h in (0, 1):
            back_copy(i, h).wait_send()
    for j in (1, 2, 3, 4):
        hs_from(j).wait_send()
        sib_copy(j).wait_send()
    for h in (0, 1):
        relay(h).wait_send()
    for copy in leaving:
        copy.wait()


def finish(*refs):
    count = len(refs) // 2
    for given, laid in zip(refs[:count], refs[count:]):
        laid[...] = given[...].reshape(laid.shape)


def per_device(queries, keys, values, out_weight, cotangent, advantages, lengths):
    rows, heads, hd = queries.shape
    width = heads * hd
    part, depth = cotangent.shape
    slices = SIDE
    fs = depth // slices
    own = depth // lax.axis_size("seq")
    q_rows = heads * rows
    vmem = pl.BlockSpec(memory_space=pltpu.VMEM)
    anywhere = pl.BlockSpec(memory_space=pl.ANY)
    smem = pl.BlockSpec(memory_space=pltpu.SMEM)
    dma = pltpu.SemaphoreType.DMA
    V = pltpu.VMEM
    out = pl.pallas_call(
        kernel,
        out_shape=[
            jax.ShapeDtypeStruct((rows, width), BF),
            jax.ShapeDtypeStruct((rows, width), BF),
            jax.ShapeDtypeStruct((rows, hd), BF),
            jax.ShapeDtypeStruct((rows, hd), BF),
            jax.ShapeDtypeStruct((own, width), F32),
        ],
        in_specs=[smem, smem] + [anywhere] * 5,
        out_specs=[anywhere] * 5,
        scratch_shapes=[
            V((rows, heads, hd), BF),
            V((part, depth), BF),
            V((rows, width), BF),
            V((rows, width), BF),
            V((rows, hd), BF),
            V((rows, hd), BF),
            V((own, width), F32),
            V((slices, rows, fs), BF),
            V((width, depth), BF),
            V((BACK + 1, rows, 2 * hd), BF),
            V((q_rows, hd), BF),
            V((hd, q_rows), BF),
            V((rows, hd), jnp.int32),
            V((BACK + 1, q_rows, rows), F32),
            V((BACK + 1, q_rows, rows), BF),
            V((q_rows, hd), F32),
            V((q_rows, hd), F32),
            V((q_rows, hd), F32),
            V((q_rows, hd), BF),
            V((rows, width), F32),
            V((q_rows, hd), BF),
            V((hd, q_rows), BF),
            V((q_rows, hd), F32),
            V((q_rows, hd), F32),
            V((q_rows, rows), BF),
            V((slices, SIDE, own, width), BF),
            V((slices, SIDE, own, width), BF),
            V((slices, SIDE, own, width), BF),
            V((slices, SIDE, own, width), BF),
            V((slices, own, width), F32),
            V((slices, own, width), BF),
            V((SIDE, own, width), BF),
            V((own, width), F32),
            V((5, 2 * hd, rows), BF),
            V((5, 2 * hd, rows), BF),
            V((4, 2 * hd, rows), BF),
            V((4, 2 * hd, rows), BF),
            V((2 * hd, rows), BF),
            V((2 * hd, rows), BF),
            dma((2, 4, slices)),
            dma((2, 4, slices)),
            dma,
            dma((2,)),
            dma((2, 4)),
            dma((2, 5)),
            dma((2, slices)),
            dma((2, slices, 4)),
            dma((slices,)),
            dma((4,)),
            dma((2, 5)),
            dma((2, 4, 2)),
            dma((2, 2)),
            dma((4,)),
            dma((5,)),
        ],
        compiler_params=pltpu.CompilerParams(
            collective_id=0, has_side_effects=True, vmem_limit_bytes=60 * 1024 * 1024
        ),
        cost_estimate=pl.CostEstimate(flops=9 * 10**9, bytes_accessed=5 * 10**6, transcendentals=5 * 10**6),
        name="rollout_attention",
    )(lengths, advantages, queries, keys.reshape(rows, hd), values.reshape(rows, hd), out_weight, cotangent)
    attention, d_queries, d_keys, d_values, d_weight = pl.pallas_call(
        finish,
        out_shape=[
            jax.ShapeDtypeStruct((rows, heads, hd), BF),
            jax.ShapeDtypeStruct((rows, heads, hd), BF),
            jax.ShapeDtypeStruct((rows, hd), BF),
            jax.ShapeDtypeStruct((rows, hd), BF),
            jax.ShapeDtypeStruct((own, width), F32),
        ],
        in_specs=[vmem] * 5,
        out_specs=[vmem] * 5,
        name="lay_out_results",
    )(*out)
    return (attention, d_queries, d_keys.reshape(rows, 1, hd), d_values.reshape(rows, 1, hd), d_weight)


def solution(mesh):
    tokens = P("seq", "tp", None)
    return jax.shard_map(
        per_device,
        mesh=mesh,
        in_specs=(tokens, tokens, tokens, P("tp", None), P(("seq", "tp"), None), P(), P()),
        out_specs=(tokens, tokens, tokens, tokens, P("seq", "tp")),
        check_vma=False,
    )
```

```python
import functools
import math

import jax
import jax.numpy as jnp
from jax import lax
from jax.experimental import pallas as pl
from jax.experimental.pallas import tpu as pltpu
from jax.sharding import PartitionSpec as P

WINDOW = 4096
SIDE = 4
RING = 8
BACK = 8
SCALE = 1.0 / 12.0
EXP2_SCALE = SCALE * math.log2(math.e)
MASKED = -1e30
BF = jnp.bfloat16
F32 = jnp.float32
MESH = pl.DeviceIdType.MESH
NN = (((1,), (0,)), ((), ()))
NT = (((1,), (1,)), ((), ()))
TN = (((0,), (0,)), ((), ()))


def dot(a, b, dims):
    return lax.dot_general(a, b, dims, preferred_element_type=F32)


def kernel(
    lens, adv, q_ref, k_ref, v_ref, w_hbm, cot_ref,
    att_o, dq_o, dk_o, dv_o, dwo_o,
    att, sc, w, kv, q2, qT, lo, hi, S, Pb, mx, rl, O2, att2,
    dA, dAs, dAsT, delta, dq, dS,
    psend, precv, ysend, yrecv, yown, xsend, xrecv, xown,
    ssend, srecv, rsend, rrecv, lsend, lrecv,
    gs_sem, gr_sem, w_sem, hx_sem, hy_sem, hs_sem,
    pp_sem, yy_sem, xs_sem, xr_sem, ss_sem, rr_sem, ll_sem,
):
    s = lax.axis_index("seq")
    z = lax.axis_index("tp")
    core = lax.rem(s, 2)
    chip = s // 2
    y = lax.rem(chip, SIDE)
    x = chip // SIDE
    rows, fs = sc.shape[1], sc.shape[2]
    ebuf = S.at[:, pl.ds(fs // 2, 2 * k_ref.shape[1]), :]
    slices = sc.shape[0]
    part = rows // RING
    hd = k_ref.shape[1]
    own_rows = dwo_o.shape[0]

    def row_dev(i):
        return {"seq": x * (2 * SIDE) + lax.rem(y + i + SIDE, SIDE) * 2 + core}

    def col_dev(i):
        return {"seq": lax.rem(x + i + SIDE, SIDE) * (2 * SIDE) + y * 2 + core}

    def ring_dev(i):
        return {"tp": lax.rem(z + i + RING, RING)}

    sib_dev = {"seq": s + 1 - 2 * core}

    def remote(src, dst, send, recv, dev):
        return pltpu.make_async_remote_copy(
            src_ref=src, dst_ref=dst, send_sem=send, recv_sem=recv, device_id=dev, device_id_type=MESH
        )

    barrier = pltpu.get_barrier_semaphore()
    next_dev = {"seq": lax.rem(s + 2, 2 * SIDE * SIDE)}
    last_dev = {"seq": lax.rem(s - 2 + 2 * SIDE * SIDE, 2 * SIDE * SIDE)}
    around = [f(i) for f in (row_dev, col_dev) for i in (1, 2, 3)]
    for dev in [sib_dev, ring_dev(1), ring_dev(-1), next_dev] + around:
        pl.semaphore_signal(barrier, inc=1, device_id=dev, device_id_type=MESH)
    w_copy = pltpu.make_async_copy(w_hbm, w, w_sem)
    w_copy.start()

    place = s * rows + z * part + lax.broadcasted_iota(jnp.int32, (part, hd), 0)
    factor = jnp.full((part, hd), adv[0], F32)
    cum = jnp.int32(0)
    for r in range(lens.shape[0] - 1):
        cum = cum + lens[r]
        factor = jnp.where(place >= cum, adv[r + 1], factor)
    wide = jnp.concatenate([factor] * (fs // hd), axis=1)
    my_rows = pl.ds(0, part)
    for f in range(slices):
        piece = cot_ref[:, f * fs : (f + 1) * fs].astype(F32)
        sc[f, my_rows, :] = (wide * piece).astype(BF)
    kv[0, :, :hd] = k_ref[...]
    kv[0, :, hd:] = v_ref[...]

    pl.semaphore_wait(barrier, 10)

    offsets = (0, 1, -1, 2, -2, 3, -3, 4)

    def chunk_of(p):
        return pl.ds(pl.multiple_of(lax.rem(z + offsets[p] + RING, RING) * part, part), part)

    def spot(away, kind, way):
        p = offsets.index(away if abs(away) < 4 else 4)
        if kind < 3:
            return pl.ds(p * part, part)
        return pl.ds(p * part + way * (part // 2), part // 2)

    def ring_copy(way, kind, f):
        sign = 1 - 2 * way
        src = sc.at[f, spot(-sign * kind, kind, way)]
        dst = sc.at[f, spot(-sign * (kind + 1), kind, way)]
        return remote(src, dst, gs_sem.at[way, kind, f], gr_sem.at[way, kind, f], ring_dev(sign))

    def arrived(kind, f):
        for way in (0, 1):
            ring_copy(way, kind, f).wait_recv()

    def event(kind, f):
        if kind:
            arrived(kind - 1, f)
        for way in (0, 1):
            ring_copy(way, kind, f).start()

    event(0, 0)
    event(0, 1)

    def hx():
        return remote(kv.at[0], kv.at[8], hx_sem.at[0], hx_sem.at[1], col_dev(1))

    hx().start()

    def hy(i, slot):
        return remote(kv.at[slot], kv.at[2 * i], hy_sem.at[0, i], hy_sem.at[1, i], row_dev(i))

    def hs(i):
        j = i + 1 - core
        return remote(kv.at[2 * i], kv.at[2 * j - 1], hs_sem.at[0, j], hs_sem.at[1, j], sib_dev)

    def hs_from(j):
        return remote(kv.at[2 * j], kv.at[2 * j - 1], hs_sem.at[0, j], hs_sem.at[1, j], sib_dev)

    for i in (1, 2, 3):
        @pl.when(y + i < SIDE)
        def _():
            hy(i, 0).start()

    @pl.when(core == 0)
    def _():
        hs(0).start()

    for p in range(RING):
        here = pl.ds(p * part, part)
        for h in range(2):
            q2[h * rows + p * part : h * rows + (p + 1) * part, :] = q_ref[chunk_of(p), h, :]
        local = lax.rem(z + offsets[p] + RING, RING) * part + lax.broadcasted_iota(jnp.int32, (part, hd), 0)
        place = s * rows + local
        first = jnp.zeros((part, hd), jnp.int32)
        cum = jnp.int32(0)
        for r in range(lens.shape[0] - 1):
            cum = cum + lens[r]
            first = jnp.where(place >= cum, cum, first)
        lo[here, :] = jnp.maximum(first, place - (WINDOW - 1)) - s * rows
        hi[here, :] = local
    qT[...] = q2[...].astype(F32).T.astype(BF)

    tile = 256
    tiles = 2 * rows // tile
    per_head = rows // tile

    def tile_rows(r):
        return pl.ds(pl.multiple_of(r * tile, tile), tile)

    def scores(d):
        def step(r, carry):
            at = tile_rows(r)
            raw = dot(q2[at, :], kv[d, :, :hd], NT)
            t0 = lax.rem(r, per_head) * tile
            low = lo[pl.ds(pl.multiple_of(t0, tile), tile), :] + d * rows
            best = None
            for c in range(rows // hd):
                col = lax.broadcasted_iota(jnp.int32, (tile, hd), 1) + c * hd
                seen = col >= low
                if d == 0:
                    seen = seen & (col <= hi[pl.ds(pl.multiple_of(t0, tile), tile), :])
                val = jnp.where(seen, raw[:, c * hd : (c + 1) * hd], MASKED)
                S[d, at, c * hd : (c + 1) * hd] = val
                best = val if best is None else jnp.maximum(best, val)
            mx[at, :] = best if d == 0 else jnp.maximum(mx[at, :], best)
            return carry

        lax.fori_loop(0, tiles, step, 0)

    def weigh(r, last):
        at = pl.ds(r * tile, tile)
        if not last:
            mx[at, :] = jnp.broadcast_to(jnp.max(mx[at, :], axis=1, keepdims=True), (tile, hd))
            rl[at, :] = jnp.zeros((tile, hd), F32)
            O2[at, :] = jnp.zeros((tile, hd), F32)

        def step(d, carry):
            top = mx[at, :]
            total = rl[at, :]
            for c in range(rows // hd):
                p = jnp.exp2((S[d, at, c * hd : (c + 1) * hd] - top) * EXP2_SCALE)
                total = total + p
                Pb[d, at, c * hd : (c + 1) * hd] = p.astype(BF)
            rl[at, :] = total
            O2[at, :] += dot(Pb[d, at, :], kv[d, :, hd:], NN)
            return carry

        middle = BACK // 2
        if not last:
            lax.fori_loop(0, middle, step, 0)
            return
        lax.fori_loop(middle, BACK + 1, step, 0)
        inv = 1.0 / jnp.broadcast_to(jnp.sum(rl[at, :], axis=1, keepdims=True), (tile, hd))
        rl[at, :] = inv
        out = (O2[at, :] * inv).astype(BF)
        att2[at, :] = out
        t0, h = (r % per_head) * tile, r // per_head
        att[t0 : t0 + tile, h * hd : (h + 1) * hd] = out
        for p in range(t0 // part, (t0 + tile) // part):
            att_o[chunk_of(p), h * hd : (h + 1) * hd] = out[p * part - t0 : (p + 1) * part - t0]

    def project(f, g=None):
        at = pl.ds(0, rows) if g is None else pl.ds(g * tile, tile)
        term = dot(sc[f, at, :], w[:, f * fs : (f + 1) * fs], NT)
        if f == 0:
            dA[at, :] = term
        else:
            dA[at, :] += term

    def pair_copy(f):
        return remote(psend.at[f], precv.at[f], pp_sem.at[0, f], pp_sem.at[1, f], sib_dev)

    def weight_rows(f, j, which):
        width = att.shape[1]
        at = pl.ds(pl.multiple_of((2 * (j % 2) + which) * own_rows, own_rows), own_rows)
        return S[BACK - f, at, (j // 2) * width : (j // 2 + 1) * width]

    def weight_grad(f):
        width = att.shape[1]
        cut = fs // 2
        for i in range(fs // hd):
            term = dot(sc[f, :, i * hd : (i + 1) * hd], att[...], TN)
            for side in (0, 1):
                first, last = max(i * hd, side * cut), min((i + 1) * hd, (side + 1) * cut)
                if first < last:
                    S[BACK - f, first - side * cut : last - side * cut, pl.ds(side * width, width)] = (
                        term[first - i * hd : last - i * hd]
                    )
        for j in range(SIDE):
            psend[f, j] = weight_rows(f, j, 1 - core).astype(BF)
        pair_copy(f).start()

    def row_copy(f, i):
        return remote(ysend.at[f, i], yrecv.at[f, i], yy_sem.at[0, f, i], yy_sem.at[1, f, i], row_dev(i))

    def row_send(f):
        pair_copy(f).wait_recv()
        for j in range(SIDE):
            both = weight_rows(f, j, core) + precv[f, j].astype(F32)
            ysend[f, lax.rem(j - y + SIDE, SIDE)] = both.astype(BF)

            @pl.when(y == j)
            def _():
                yown[f] = both

        for i in (1, 2, 3):
            row_copy(f, i).start()

    def col_copy(f):
        slot = lax.rem(x - f + SIDE, SIDE)
        return remote(
            xsend.at[f], xrecv.at[slot], xs_sem.at[f], xr_sem.at[slot],
            {"seq": f * (2 * SIDE) + y * 2 + core},
        )

    def col_from(i):
        return remote(xsend.at[i], xrecv.at[i], xs_sem.at[i], xr_sem.at[i], col_dev(i))

    def col_send(f):
        total = yown[f]
        for i in (1, 2, 3):
            row_copy(f, i).wait_recv()
            total = total + yrecv[f, i].astype(F32)

        @pl.when(x == f)
        def _():
            xown[...] = total

        @pl.when(x != f)
        def _():
            xsend[f] = total.astype(BF)
            col_copy(f).start()

    def ready(g):
        for h in range(2):
            at = pl.ds(h * rows + g * tile, tile)
            rounded = dA[pl.ds(g * tile, tile), h * hd : (h + 1) * hd].astype(BF).astype(F32)
            scaled = (rounded * rl[at, :]).astype(BF)
            dAs[at, :] = scaled
            wide = scaled.astype(F32)
            dAsT[:, at] = wide.T.astype(BF)
            d = jnp.sum(wide * att2[at, :].astype(F32), axis=1, keepdims=True)
            delta[at, :] = jnp.broadcast_to(d, (tile, hd))

    def backward(d, g, out, first=False):
        dk_part, dv_part = 0.0, 0.0
        for h in range(2):
            at = pl.ds(h * rows + g * tile, tile)
            raw = dot(dAs[at, :], kv[d, :, hd:], NT)
            low = delta[at, :]
            for c in range(rows // hd):
                cs = slice(c * hd, (c + 1) * hd)
                dS[at, cs] = (Pb[d, at, cs].astype(F32) * (raw[:, cs] - low)).astype(BF)
            term = dot(dS[at, :], kv[d, :, :hd], NN)
            if first:
                dq[at, :] = term
            else:
                dq[at, :] += term
            dk_part += dot(qT[:, at], dS[at, :], NN)
            dv_part += dot(dAsT[:, at], Pb[d, at, :], NN)
        if g:
            dk_part, dv_part = ebuf[d, :hd, :] + dk_part, ebuf[d, hd:, :] + dv_part
        out[:hd, :] = dk_part.astype(out.dtype)
        out[hd:, :] = dv_part.astype(out.dtype)

    def early(d, first=False):
        backward(d, 0, ebuf.at[d], first)

    def sib_copy(i):
        return remote(ssend.at[i], srecv.at[i], ss_sem.at[0, i], ss_sem.at[1, i], sib_dev)

    def half(ref, h):
        return ref.at[pl.ds(h * hd, hd)]

    def back_copy(i, h):
        dev = last_dev if i == 1 else row_dev(-i)
        return remote(half(rsend.at[i], h), half(rrecv.at[i], h), rr_sem.at[0, i, h], rr_sem.at[1, i, h], dev)

    def relay(h):
        return remote(half(lsend, h), half(lrecv, h), ll_sem.at[0, h], ll_sem.at[1, h], col_dev(-1))

    def odd(i, first=False):
        backward(2 * i - 1, 1, ssend.at[i], first)
        sib_copy(i).start()

    def send_back(i):
        j = i + 1 - core
        sib_copy(j).wait_recv()
        for h in (0, 1):
            hs_ = pl.ds(h * hd, hd)
            rsend[i, hs_, :] = (ebuf[2 * i, hs_, :] + srecv[j, hs_, :].astype(F32)).astype(BF)
            back_copy(i, h).start()

    def relay_in():
        hx().wait_recv()
        for i in (1, 2, 3):
            @pl.when(y + i >= SIDE)
            def _():
                hy(i, 8).start()

        @pl.when(core == 1)
        def _():
            hs(4).start()

    def even_in(i):
        hy(i, 0).wait_recv()
        hs(i).start()
        scores(2 * i)

    def odd_in(j):
        hs_from(j).wait_recv()
        scores(2 * j - 1)

    scores(0)
    event(1, 0)
    event(0, 2)
    relay_in()
    scores(8)
    event(1, 1)
    event(2, 0)
    even_in(1)
    event(2, 1)
    event(1, 2)
    odd_in(1)
    even_in(3)
    event(3, 0)
    event(0, 3)
    even_in(2)
    odd_in(2)
    odd_in(3)
    event(3, 1)
    odd_in(4)
    weigh(0, False)
    weigh(0, True)
    event(2, 2)
    weigh(1, False)
    weigh(1, True)
    w_copy.wait()
    arrived(3, 0)
    project(0)
    weigh(2, False)
    weigh(2, True)
    event(1, 3)
    weigh(3, False)
    arrived(3, 1)
    project(1)
    weigh(3, True)
    weight_grad(0)
    event(3, 2)
    project(2, 0)
    weight_grad(1)
    row_send(0)
    event(2, 3)
    project(3, 0)
    ready(0)
    early(7, True)
    row_send(1)
    early(5)
    early(6)
    arrived(3, 2)
    project(2, 1)
    event(3, 3)
    weight_grad(2)
    early(3)
    early(4)
    row_send(2)
    early(1)
    col_send(0)
    early(8)
    early(2)
    early(0)
    arrived(3, 3)
    project(3, 1)
    ready(1)
    weight_grad(3)
    odd(4, True)
    row_send(3)
    odd(3)
    backward(6, 1, ebuf.at[6])
    send_back(3)
    odd(2)
    backward(4, 1, ebuf.at[4])
    send_back(2)
    odd(1)
    backward(2, 1, ebuf.at[2])
    send_back(1)
    backward(8, 1, ebuf.at[8])
    col_send(1)
    backward(0, 1, ebuf.at[0])
    col_send(2)
    col_send(3)
    for p in range(RING):
        for h in range(2):
            grad = dq[pl.ds(h * rows + p * part, part), :] * SCALE
            dq_o[chunk_of(p), h * hd : (h + 1) * hd] = grad.astype(BF)

    @pl.when(core == 1)
    def _():
        sib_copy(4).wait_recv()

    for h in (0, 1):
        hr = pl.ds(h * hd, hd)
        total = ebuf[8, hr, :] + jnp.where(core == 1, srecv[4, hr, :].astype(F32), 0.0)
        for i in (3, 2):
            back_copy(i, h).wait_recv()
            total = total + jnp.where(y + i >= SIDE, rrecv[i, hr, :].astype(F32), 0.0)
        lsend[hr, :] = total.astype(BF)
        relay(h).start()
    own = xown[...]
    for i in (1, 2, 3):
        col_from(i).wait_recv()
        own = own + xrecv[i].astype(F32)
    dwo_o[...] = own

    @pl.when(core == 0)
    def _():
        sib_copy(1).wait_recv()

    for h in (0, 1):
        hr = pl.ds(h * hd, hd)
        total = ebuf[0, hr, :] + jnp.where(core == 0, srecv[1, hr, :].astype(F32), 0.0)
        for i in (3, 2):
            total = total + jnp.where(y + i < SIDE, rrecv[i, hr, :].astype(F32), 0.0)
        back_copy(1, h).wait_recv()
        total = total + rrecv[1, hr, :].astype(F32)
        relay(h).wait_recv()
        total = total + lrecv[hr, :].astype(F32)
        if h == 0:
            dk_o[...] = (total.T * SCALE).astype(BF)
        else:
            dv_o[...] = total.T.astype(BF)

    for f in range(slices):
        for way in (0, 1):
            for kind in range(4):
                ring_copy(way, kind, f).wait_send()
        pair_copy(f).wait_send()
        for i in (1, 2, 3):
            row_copy(f, i).wait_send()

        @pl.when(x != f)
        def _():
            col_copy(f).wait_send()
    hx().wait_send()
    for i in (1, 2, 3):
        hy(i, 0).wait_send()
        for h in (0, 1):
            back_copy(i, h).wait_send()
    for j in (1, 2, 3, 4):
        hs_from(j).wait_send()
        sib_copy(j).wait_send()
    for h in (0, 1):
        relay(h).wait_send()


def finish(*refs):
    count = len(refs) // 2
    for given, laid in zip(refs[:count], refs[count:]):
        laid[...] = given[...].reshape(laid.shape)


def per_device(queries, keys, values, out_weight, cotangent, advantages, lengths):
    rows, heads, hd = queries.shape
    width = heads * hd
    depth = cotangent.shape[1]
    slices = SIDE
    fs = depth // slices
    own = depth // lax.axis_size("seq")
    q_rows = heads * rows
    vmem = pl.BlockSpec(memory_space=pltpu.VMEM)
    anywhere = pl.BlockSpec(memory_space=pl.ANY)
    smem = pl.BlockSpec(memory_space=pltpu.SMEM)
    dma = pltpu.SemaphoreType.DMA
    V = pltpu.VMEM
    out = pl.pallas_call(
        kernel,
        out_shape=[
            jax.ShapeDtypeStruct((rows, width), BF),
            jax.ShapeDtypeStruct((rows, width), BF),
            jax.ShapeDtypeStruct((rows, hd), BF),
            jax.ShapeDtypeStruct((rows, hd), BF),
            jax.ShapeDtypeStruct((own, width), F32),
        ],
        in_specs=[smem, smem, vmem, vmem, vmem, anywhere, vmem],
        out_specs=[vmem] * 5,
        scratch_shapes=[
            V((rows, width), BF),
            V((slices, rows, fs), BF),
            V((width, depth), BF),
            V((BACK + 1, rows, 2 * hd), BF),
            V((q_rows, hd), BF),
            V((hd, q_rows), BF),
            V((rows, hd), jnp.int32),
            V((rows, hd), jnp.int32),
            V((BACK + 1, q_rows, rows), F32),
            V((BACK + 1, q_rows, rows), BF),
            V((q_rows, hd), F32),
            V((q_rows, hd), F32),
            V((q_rows, hd), F32),
            V((q_rows, hd), BF),
            V((rows, width), F32),
            V((q_rows, hd), BF),
            V((hd, q_rows), BF),
            V((q_rows, hd), F32),
            V((q_rows, hd), F32),
            V((q_rows, rows), BF),
            V((slices, SIDE, own, width), BF),
            V((slices, SIDE, own, width), BF),
            V((slices, SIDE, own, width), BF),
            V((slices, SIDE, own, width), BF),
            V((slices, own, width), F32),
            V((slices, own, width), BF),
            V((SIDE, own, width), BF),
            V((own, width), F32),
            V((5, 2 * hd, rows), BF),
            V((5, 2 * hd, rows), BF),
            V((4, 2 * hd, rows), BF),
            V((4, 2 * hd, rows), BF),
            V((2 * hd, rows), BF),
            V((2 * hd, rows), BF),
            dma((2, 4, slices)),
            dma((2, 4, slices)),
            dma,
            dma((2,)),
            dma((2, 4)),
            dma((2, 5)),
            dma((2, slices)),
            dma((2, slices, 4)),
            dma((slices,)),
            dma((4,)),
            dma((2, 5)),
            dma((2, 4, 2)),
            dma((2, 2)),
        ],
        compiler_params=pltpu.CompilerParams(
            collective_id=0, has_side_effects=True, vmem_limit_bytes=60 * 1024 * 1024
        ),
        cost_estimate=pl.CostEstimate(flops=9 * 10**9, bytes_accessed=5 * 10**6, transcendentals=5 * 10**6),
        name="rollout_attention",
    )(lengths, advantages, queries, keys.reshape(rows, hd), values.reshape(rows, hd), out_weight, cotangent)
    attention, d_queries, d_keys, d_values, d_weight = pl.pallas_call(
        finish,
        out_shape=[
            jax.ShapeDtypeStruct((rows, heads, hd), BF),
            jax.ShapeDtypeStruct((rows, heads, hd), BF),
            jax.ShapeDtypeStruct((rows, hd), BF),
            jax.ShapeDtypeStruct((rows, hd), BF),
            jax.ShapeDtypeStruct((own, width), F32),
        ],
        in_specs=[vmem] * 5,
        out_specs=[vmem] * 5,
        name="lay_out_results",
    )(*out)
    return (attention, d_queries, d_keys.reshape(rows, 1, hd), d_values.reshape(rows, 1, hd), d_weight)


def solution(mesh):
    tokens = P("seq", "tp", None)
    return jax.shard_map(
        per_device,
        mesh=mesh,
        in_specs=(tokens, tokens, tokens, P("tp", None), P(("seq", "tp"), None), P(), P()),
        out_specs=(tokens, tokens, tokens, tokens, P("seq", "tp")),
        check_vma=False,
    )
```
